32 devices in a mesh: groups: 2 (over x), angle: 8 (over z, y), tile: 2 (over core).
Axes of the slice: x: 2, y: 2, z: 4, core: 2. Of those that a mesh axis runs over, the one named last changes fastest.
Arguments:
- intensity: float32 [128, 128, 2048], P(('groups', 'angle', 'tile')), parts along dimension 0, may hold values from 0.2 to 1
- counts: int32 [16], P('groups'), parts along dimension 0, may hold values from 1 to 32, 128 in all
- segment_ids: int32 [64, 64], replicated, may hold values from 0 to 15
- tile_ids: int32 [64, 64], replicated, may hold values from 0 to 15
- block_order: int32 [128], P('groups'), parts along dimension 0, may hold values from 0 to 63, each once
- tiles: bfloat16 [16, 128, 128], replicated, may hold values from -0.0625 to 0.0625
Outputs:
- volume: float32 [16, 32, 64, 128], P(('groups', 'angle'), None, 'tile'), parts along dimension 0
The draws below stay inside these ranges and needn't reach their ends.
There are 2 independent parts, one for each index of `groups`. The reference program is written for one: setup_inputs(seed, part) draws one part's arguments, and reference() takes and returns one part's arrays. A program takes and returns all parts, laid end to end along the dimension named above; an argument that names none is the same for every part. Nothing has to cross between parts.
Inputs may be any that keep to these rules, and one draw needn't show every extreme that they name: Slice group g takes counts[g] consecutive detector rows, groups in order; the counts sum to 128 and the largest is exactly 32. `block_order`: each voxel block appears once.
All inputs are finite; a program needn't handle non-finite values.
Results may differ from the reference program's by a relative error of at most 0.00075.
Values may be sent and summed in bfloat16 or wider, within the bound.
A program may use at most 128 MiB of HBM per device.

```python
import math
import jax
import jax.numpy as jnp
import numpy as np
from jax import lax

ROWS = 128
W = 2048
VOX = 128
NT = 16
ANGLES = 64
GMAX = 32
NB = 64
SEGS = 16
N_ANGLE = 8


def touch_ends(result, rng, low, largest):
    place = [jax.random.randint(jax.random.fold_in(rng, axis), (), 0, length) for axis, length in enumerate(result.shape)]
    main_axis = result.shape.index(max(result.shape))
    next_to = place[:main_axis] + [(place[main_axis] + 1) % result.shape[main_axis]] + place[main_axis + 1:]
    return result.at[tuple(place)].set(low).at[tuple(next_to)].set(largest)


def level_of(rng, shape, cuts, least, largest):
    def one(axis_at, shards_of):
        steps = jax.random.uniform(jax.random.fold_in(jax.random.fold_in(rng, 6), axis_at), (shards_of,), jnp.float32, least / len(cuts), largest / len(cuts))
        return jnp.repeat(jnp.exp(steps), shape[axis_at] // shards_of).reshape((-1,) + (1,) * (len(shape) - axis_at - 1))

    gain = one(*cuts[0])
    for cut in cuts[1:]:
        gain = gain * one(*cut)
    return gain


def split_up(number_of, total, reach, lean):
    weights = [(1 << 20) // math.isqrt(grade ** lean) + 1 for grade in range(2, number_of + 1)]
    spare, given = total - reach - (number_of - 1), [1] * (number_of - 1)
    while spare > 0:
        candidates = [i for i in range(number_of - 1) if given[i] < reach]
        pool, left = sum([weights[i] for i in candidates]), spare
        for i in candidates:
            addition = min(reach - given[i], max(1, left * weights[i] // pool), spare)
            given[i] = given[i] + addition
            spare = spare - addition
    return np.array([reach] + given)


def ragged_sizes(stream_key, count, total, most, lean):
    if count == 2:
        one = jax.random.randint(stream_key, (), max(1, total - most), min(most, total - 1) + 1)
        return jnp.stack([one, total - one])
    sizes = jnp.asarray(split_up(count, total, most, lean), jnp.int32)
    couples = (count - 1) // 2
    donor, taker = sizes[1:1 + 2 * couples:2], sizes[2:2 + 2 * couples:2]
    slack = jnp.minimum(donor - 1, most - taker)
    passed = jax.random.randint(jax.random.fold_in(stream_key, 1), (couples,), 0, 1 << 20) % (slack + 1)
    sizes = sizes.at[1:1 + 2 * couples:2].set(donor - passed).at[2:2 + 2 * couples:2].set(taker + passed)
    return sizes[jax.random.permutation(jax.random.fold_in(stream_key, 2), count)]


def centred(key, extent, spread, limit, kind=jnp.bfloat16):
    return jnp.clip(spread * jax.random.normal(key, extent, jnp.float32), -limit, limit).astype(kind)


def setup_inputs(seed: int = 0, part: int = 0) -> dict:
    key_of = jax.random.split(jax.random.key(seed), 7)
    part_keys = jax.random.split(jax.random.fold_in(key_of[6], part), 7)
    intensity = jnp.clip(0.2 + 0.8 * jax.random.uniform(part_keys[0], (ANGLES, ROWS, W), jnp.float32) ** level_of(part_keys[0], (ANGLES, ROWS, W), ((0, 16),), -0.2, 0.2), 0.2, 1.0)
    counts = ragged_sizes(part_keys[1], N_ANGLE, ROWS, GMAX, 2).astype(jnp.int32)
    segment_ids = touch_ends(jax.random.randint(key_of[2], (ANGLES, NB), 0, SEGS), jax.random.fold_in(key_of[2], 1), 0, SEGS - 1).astype(jnp.int32)
    tile_ids = touch_ends(jax.random.randint(key_of[3], (ANGLES, NB), 0, NT), jax.random.fold_in(key_of[3], 1), 0, NT - 1).astype(jnp.int32)
    block_order = jax.random.permutation(part_keys[4], NB).astype(jnp.int32)
    tiles = centred(key_of[5], (NT, VOX, VOX), (VOX * ANGLES) ** -0.5, 0.0625)
    return {"intensity": intensity, "counts": counts, "segment_ids": segment_ids, "tile_ids": tile_ids, "block_order": block_order, "tiles": tiles}


paganin_alpha = 2.0


def reference(intensity, counts, segment_ids, tile_ids, block_order, tiles):
    row_freq = jnp.arange(ROWS).astype(jnp.float32)
    col_freq = jnp.arange(W).astype(jnp.float32)
    row_weight = 4.0 * jnp.square(jnp.sin(jnp.pi * row_freq / ROWS))
    col_weight = 4.0 * jnp.square(jnp.sin(jnp.pi * col_freq / W))
    weight = 1.0 / (1.0 + paganin_alpha * (row_weight[:, None] + col_weight[None, :]))

    def filter_one(projection):
        spectrum = jnp.fft.fft2(projection)
        return jnp.real(jnp.fft.ifft2(spectrum * weight))

    filtered = lax.map(filter_one, intensity)
    thickness = (-jnp.log(filtered)).astype(jnp.bfloat16)
    seg_ordered = jnp.take(segment_ids, block_order, axis=1)
    tile_ordered = jnp.take(tile_ids, block_order, axis=1)
    onehot = (tile_ordered[:, :, None] == jnp.arange(NT, dtype=jnp.int32)[None, None, :]).astype(jnp.float32)
    tiles_wide = tiles.astype(jnp.float32)

    def one_row(row_slices):
        pieces = row_slices.astype(jnp.float32).reshape(ANGLES, W // VOX, VOX)
        chosen = jnp.take_along_axis(pieces, seg_ordered[:, :, None], axis=1)
        grouped = jnp.einsum('avc,avx->vcx', onehot, chosen, precision=lax.Precision.HIGHEST)
        return jnp.einsum('vcx,cxy->vy', grouped, tiles_wide, precision=lax.Precision.HIGHEST)

    voxel_rows = lax.map(one_row, jnp.swapaxes(thickness, 0, 1))
    starts = (jnp.cumsum(counts) - counts).astype(jnp.int32)
    slot_index = jnp.arange(GMAX, dtype=jnp.int32)
    row_index = jnp.minimum(starts[:, None] + slot_index[None, :], ROWS - 1).astype(jnp.int32)
    slot_valid = slot_index[None, :] < counts[:, None]
    gathered = jnp.take(voxel_rows, row_index.reshape(-1), axis=0).reshape(N_ANGLE, GMAX, NB, VOX)
    return jnp.where(slot_valid[:, :, None, None], gathered, jnp.zeros((), jnp.float32))
```

```python
import functools
import math

import jax
import jax.numpy as jnp
import numpy as np
from jax import lax
from jax.experimental import pallas as pl
from jax.experimental.pallas import tpu as pltpu
from jax.sharding import PartitionSpec as P

paganin_alpha = 2.0
link_type = jnp.float16
chunk_total = 4


def split_pair(array):
    high = array.astype(jnp.bfloat16)
    low = (array - high.astype(jnp.float32)).astype(jnp.bfloat16)
    return high, low


def filter_tables(row_total):
    index = np.arange(row_total)
    phase = 2.0 * np.pi * (index[:, None] * index[None, :] % row_total) / row_total
    hartley = (np.cos(phase) + np.sin(phase)) / math.sqrt(row_total)
    high = hartley.astype(np.float32).astype(jnp.bfloat16)
    low = (hartley - high.astype(np.float64)).astype(np.float32).astype(jnp.bfloat16)
    a = 1.0 + paganin_alpha * (4.0 * np.sin(np.pi * index / row_total) ** 2 + 2.0)
    pole = (a - np.sqrt(a * a - 4.0 * paganin_alpha**2)) / (2.0 * paganin_alpha)
    gain = pole / (paganin_alpha * (1.0 - pole * pole))
    forward = np.concatenate([np.concatenate([high, low], 1)] * 2, 0)
    inverse = np.concatenate([np.concatenate([high, high], 1), np.concatenate([low, low], 1)], 0)
    poles = np.stack([pole, gain]).astype(np.float32)
    return forward, inverse, poles


def filter_kernel(x_ref, forward_ref, inverse_ref, pole_ref, out_ref, spectrum, causal):
    edge = out_ref.shape[-1]
    segments = out_ref.shape[1]
    rows = out_ref.shape[2]
    for s in range(segments):
        high, low = split_pair(x_ref[0, :, s * edge : (s + 1) * edge])
        both = jnp.concatenate([high, low], axis=0)
        product = lax.dot_general(
            both, forward_ref[...], (((0,), (0,)), ((), ())), preferred_element_type=jnp.float32
        )
        spectrum[s * edge : (s + 1) * edge, :] = product[:, :rows] + product[:, rows:]
    pole = jnp.broadcast_to(pole_ref[0:1, :], (segments, rows))
    gain = jnp.broadcast_to(pole_ref[1:2, :], (segments, rows))
    zero = jnp.zeros((segments, rows), jnp.float32)

    def column(t):
        return pl.ds(t, segments, stride=edge)

    def warm(t, state):
        ahead, behind = state
        return (
            ahead * pole + spectrum[column(t), :],
            behind * pole + spectrum[column(edge - 1 - t), :],
        )

    ahead, behind = lax.fori_loop(0, edge, warm, (zero, zero), unroll=8)
    ahead = jnp.concatenate([ahead[segments - 1 :], ahead[: segments - 1]], axis=0)
    behind = jnp.concatenate([behind[1:], behind[:1]], axis=0)

    def sweep(t, state):
        ahead, behind = state
        ahead = ahead * pole + spectrum[column(t), :]
        causal[0, column(t), :] = ahead * gain
        back = edge - 1 - t
        behind = behind * pole
        causal[1, column(back), :] = behind * gain
        return ahead, behind + spectrum[column(back), :]

    lax.fori_loop(0, edge, sweep, (ahead, behind), unroll=8)
    for s in range(segments):
        span = slice(s * edge, (s + 1) * edge)
        high, low = split_pair(causal[0, span, :] + causal[1, span, :])
        both = jnp.concatenate([high, low], axis=1)
        product = lax.dot_general(
            inverse_ref[...], both, (((1,), (1,)), ((), ())), preferred_element_type=jnp.float32
        )
        out_ref[0, s] = (-jnp.log(product[:rows] + product[rows:])).astype(jnp.bfloat16)


def paganin_thickness(intensity, edge):
    angles, rows, width = intensity.shape
    forward, inverse, poles = filter_tables(rows)
    segments = width // edge
    whole = lambda *shape: pl.BlockSpec(shape, lambda a: (0,) * len(shape))
    return pl.pallas_call(
        filter_kernel,
        grid=(angles,),
        out_shape=jax.ShapeDtypeStruct((angles, segments, rows, edge), jnp.bfloat16),
        in_specs=[
            pl.BlockSpec((1, rows, width), lambda a: (a, 0, 0)),
            whole(2 * rows, 2 * rows),
            whole(2 * rows, 2 * rows),
            whole(2, rows),
        ],
        out_specs=pl.BlockSpec((1, segments, rows, edge), lambda a: (a, 0, 0, 0)),
        scratch_shapes=[
            pltpu.VMEM((width, rows), jnp.float32),
            pltpu.VMEM((2, width, rows), jnp.float32),
        ],
        compiler_params=pltpu.CompilerParams(vmem_limit_bytes=32 * 2**20),
        name="paganin_filter",
    )(intensity, jnp.asarray(forward), jnp.asarray(inverse), jnp.asarray(poles))


def backproject_kernel(first, seg_ref, tile_ref, order_ref, start_ref, count_ref, *refs):
    *thick_refs, tiles_ref, out_ref, rows_ref = refs
    groups, block_total, capacity, edge = out_ref.shape
    angles, _, rows, _ = thick_refs[0].shape
    rows_ref[rows:, :] = jnp.zeros((rows_ref.shape[0] - rows, edge), jnp.float32)
    slot = lax.broadcasted_iota(jnp.int32, (capacity, edge), 0)

    def one_block(v, _):
        block = order_ref[first + v]
        pieces, maps = [], []
        for source, thick in enumerate(thick_refs):
            for a in range(angles):
                row = source * angles + a
                pieces.append(thick[a, seg_ref[row, block]])
                maps.append(tiles_ref[tile_ref[row, block]])
        rows_ref[:rows, :] = jnp.dot(
            jnp.concatenate(pieces, axis=1),
            jnp.concatenate(maps, axis=0),
            preferred_element_type=jnp.float32,
        )
        for g in range(groups):
            picked = rows_ref[pl.ds(start_ref[g], capacity), :]
            out_ref[g, v] = jnp.where(slot < count_ref[g], picked, 0.0)
        return 0

    lax.fori_loop(0, block_total, one_block, 0)


def backproject(thick, seg_rows, tile_rows, order, starts, counts, tiles, first, blocks, capacity):
    angles, segments, rows, edge = thick[0].shape
    groups = starts.shape[0]
    smem = pl.BlockSpec(memory_space=pltpu.SMEM)
    vmem = pl.BlockSpec(memory_space=pltpu.VMEM)
    flops = 2 * len(thick) * angles * blocks * rows * edge * edge
    return pl.pallas_call(
        functools.partial(backproject_kernel, first),
        out_shape=jax.ShapeDtypeStruct((groups, blocks, capacity, edge), jnp.float32),
        in_specs=[smem] * 5 + [vmem] * (len(thick) + 1),
        out_specs=vmem,
        scratch_shapes=[pltpu.VMEM((rows + capacity, edge), jnp.float32)],
        compiler_params=pltpu.CompilerParams(vmem_limit_bytes=32 * 2**20),
        cost_estimate=pl.CostEstimate(
            flops=flops, bytes_accessed=4 * groups * blocks * capacity * edge, transcendentals=0
        ),
        name="backproject",
    )(seg_rows, tile_rows, order, starts, counts, *thick, tiles)


def butterfly(partial, scale, lead):
    total = partial.shape[0]
    bits = total.bit_length() - 1
    remaining = list(range(bits - 1, -1, -1))
    current = partial.reshape((2,) * bits + partial.shape[1:])
    order = list(range(bits))
    if bits > 1 and lead:
        order[0], order[1] = order[1], order[0]
    for bit in order:
        axis = remaining.index(bit)
        remaining.remove(bit)
        keep = lax.index_in_dim(current, 0, axis, keepdims=False)
        send = lax.index_in_dim(current, 1, axis, keepdims=False)
        pairs = [(i, i ^ (1 << bit)) for i in range(total)]
        came = lax.ppermute((send * scale).astype(link_type), "angle", pairs)
        current = keep + came.astype(jnp.float32) / scale
    return current


def per_device(intensity, counts, segment_ids, tile_ids, block_order, tiles):
    angles, rows, _ = intensity.shape
    edge = tiles.shape[1]
    groups = lax.axis_size("angle")
    cores = lax.axis_size("tile")
    place = lax.axis_index("angle")
    core = lax.axis_index("tile")
    capacity = 2 * rows // groups
    blocks = block_order.shape[0] // cores
    angle_total = segment_ids.shape[0]

    thickness = paganin_thickness(intensity, edge)
    thick, angle_rows = [thickness], [(place * cores + core) * angles]
    for step in range(1, cores):
        pairs = [(i, (i + step) % cores) for i in range(cores)]
        thick.append(lax.ppermute(thickness, "tile", pairs))
        angle_rows.append((place * cores + (core - step) % cores) * angles)

    seg_rows = jnp.concatenate(
        [lax.dynamic_slice_in_dim(segment_ids, row, angles) for row in angle_rows]
    )
    tile_rows = jnp.concatenate(
        [lax.dynamic_slice_in_dim(tile_ids, row, angles) for row in angle_rows]
    )
    order = lax.dynamic_slice_in_dim(block_order, core * blocks, blocks)
    relative = jnp.arange(groups, dtype=jnp.int32)
    member = relative[None, :] == (relative ^ place)[:, None]
    before = relative[None, :] < (relative ^ place)[:, None]
    near_counts = jnp.sum(jnp.where(member, counts[None, :], 0), axis=1)
    near_starts = jnp.sum(jnp.where(before, counts[None, :], 0), axis=1)

    largest = jnp.max(jnp.abs(tiles.astype(jnp.float32)))
    bound = 1.75 * angle_total * edge * jnp.where(largest > 0.0, largest, 1.0)
    scale = 60000.0 / bound

    chunks = math.gcd(chunk_total, blocks)
    per_chunk = blocks // chunks
    finished = []
    for c in range(chunks):
        partial = backproject(
            thick, seg_rows, tile_rows, order, near_starts, near_counts, tiles,
            c * per_chunk, per_chunk, capacity,
        )
        finished.append(butterfly(partial, scale, c % 2))
    volume = jnp.concatenate(finished, axis=0)
    return jnp.swapaxes(volume, 0, 1)[None]


def solution(mesh):
    in_specs = (P(("groups", "angle", "tile"), None, None), P("groups"), P(), P(), P("groups"), P())
    out_specs = P(("groups", "angle"), None, "tile", None)
    return jax.shard_map(
        per_device, mesh=mesh, in_specs=in_specs, out_specs=out_specs, check_vma=False
    )
```

```python
import functools
import math

import jax
import jax.numpy as jnp
import numpy as np
from jax import lax
from jax.experimental import pallas as pl
from jax.experimental.pallas import tpu as pltpu
from jax.sharding import PartitionSpec as P

paganin_alpha = 2.0
link_type = jnp.float16
chunk_total = 4
pitch_extra = 9
unroll_blocks = 4


def split_pair(array):
    high = array.astype(jnp.bfloat16)
    low = (array - high.astype(jnp.float32)).astype(jnp.bfloat16)
    return high, low


def filter_tables(row_total, edge):
    index = np.arange(row_total)
    phase = 2.0 * np.pi * (index[:, None] * index[None, :] % row_total) / row_total
    hartley = (np.cos(phase) + np.sin(phase)) / math.sqrt(row_total)
    a = 1.0 + paganin_alpha * (4.0 * np.sin(np.pi * index / row_total) ** 2 + 2.0)
    pole = (a - np.sqrt(a * a - 4.0 * paganin_alpha**2)) / (2.0 * paganin_alpha)
    gain = pole / (paganin_alpha * (1.0 - pole * pole))

    def halves(matrix):
        high = matrix.astype(np.float32).astype(jnp.bfloat16)
        return high, (matrix - high.astype(np.float64)).astype(np.float32).astype(jnp.bfloat16)

    high, low = halves(hartley * gain[None, :])
    forward = np.concatenate([np.concatenate([high, low], 1)] * 2, 0)
    high, low = halves(hartley)
    inverse = np.concatenate([np.concatenate([high, high], 1), np.concatenate([low, low], 1)], 0)
    reach = pole[None, :] ** np.arange(1, edge + 1)[:, None]
    powers = np.concatenate([reach, reach[::-1]], 0).astype(np.float32)
    return forward, inverse, powers


def filter_kernel(x_ref, forward_ref, inverse_ref, power_ref, out_ref, spectrum, ahead_ref, behind_ref, ends):
    edge = out_ref.shape[-1]
    segments = out_ref.shape[1]
    rows = out_ref.shape[2]
    pitch = edge + pitch_extra
    for s in range(segments):
        high, low = split_pair(x_ref[0, :, s * edge : (s + 1) * edge])
        both = jnp.concatenate([high, low], axis=0)
        product = lax.dot_general(
            both, forward_ref[...], (((0,), (0,)), ((), ())), preferred_element_type=jnp.float32
        )
        spectrum[s * pitch : s * pitch + edge, :] = product[:, :rows] + product[:, rows:]
    pole = jnp.broadcast_to(power_ref[0:1, :], (segments, rows))
    zero = jnp.zeros((segments, rows), jnp.float32)

    def column(t):
        return pl.ds(t, segments, stride=pitch)

    def sweep(t, state):
        ahead, behind = state
        ahead = ahead * pole + spectrum[column(t), :]
        ahead_ref[column(t), :] = ahead
        back = edge - 1 - t
        behind = behind * pole
        behind_ref[column(back), :] = behind
        return ahead, behind + spectrum[column(back), :]

    ahead, behind = lax.fori_loop(0, edge, sweep, (zero, zero), unroll=16)
    ends[0] = ahead
    ends[1] = behind
    for s in range(segments):
        span = slice(s * pitch, s * pitch + edge)
        before, after = (s - 1) % segments, (s + 1) % segments
        value = ahead_ref[span, :] + behind_ref[span, :]
        value = value + power_ref[:edge, :] * ends[0, before : before + 1, :]
        value = value + power_ref[edge:, :] * ends[1, after : after + 1, :]
        high, low = split_pair(value)
        both = jnp.concatenate([high, low], axis=1)
        product = lax.dot_general(
            inverse_ref[...], both, (((1,), (1,)), ((), ())), preferred_element_type=jnp.float32
        )
        out_ref[0, s] = (-jnp.log(product[:rows] + product[rows:])).astype(jnp.bfloat16)


def paganin_thickness(intensity, edge):
    angles, rows, width = intensity.shape
    forward, inverse, powers = filter_tables(rows, edge)
    segments = width // edge
    whole = lambda *shape: pl.BlockSpec(shape, lambda a: (0,) * len(shape))
    plane = pltpu.VMEM((segments * (edge + pitch_extra), rows), jnp.float32)
    return pl.pallas_call(
        filter_kernel,
        grid=(angles,),
        out_shape=jax.ShapeDtypeStruct((angles, segments, rows, edge), jnp.bfloat16),
        in_specs=[
            pl.BlockSpec((1, rows, width), lambda a: (a, 0, 0)),
            whole(2 * rows, 2 * rows),
            whole(2 * rows, 2 * rows),
            whole(2 * edge, rows),
        ],
        out_specs=pl.BlockSpec((1, segments, rows, edge), lambda a: (a, 0, 0, 0)),
        scratch_shapes=[plane, plane, plane, pltpu.VMEM((2, segments, rows), jnp.float32)],
        compiler_params=pltpu.CompilerParams(vmem_limit_bytes=60 * 2**20),
        name="paganin_filter",
    )(intensity, jnp.asarray(forward), jnp.asarray(inverse), jnp.asarray(powers))


def backproject_kernel(first, seg_ref, tile_ref, order_ref, start_ref, count_ref, *refs):
    *thick_refs, tiles_ref, out_ref, rows_ref = refs
    groups, block_total, capacity, edge = out_ref.shape
    angles, _, rows, _ = thick_refs[0].shape
    lanes = math.gcd(unroll_blocks, block_total)
    for lane in range(lanes):
        rows_ref[lane, rows:, :] = jnp.zeros((capacity, edge), jnp.float32)
    slot = lax.broadcasted_iota(jnp.int32, (capacity, edge), 0)

    def some_blocks(step, _):
        for lane in range(lanes):
            v = step * lanes + lane
            block = order_ref[first + v]
            pieces, maps = [], []
            for source, thick in enumerate(thick_refs):
                for a in range(angles):
                    row = source * angles + a
                    pieces.append(thick[a, seg_ref[row, block]])
                    maps.append(tiles_ref[tile_ref[row, block]])
            rows_ref[lane, :rows, :] = jnp.dot(
                jnp.concatenate(pieces, axis=1),
                jnp.concatenate(maps, axis=0),
                preferred_element_type=jnp.float32,
            )
            for g in range(groups):
                picked = rows_ref[lane, pl.ds(start_ref[g], capacity), :]
                out_ref[g, v] = jnp.where(slot < count_ref[g], picked, 0.0)
        return 0

    lax.fori_loop(0, block_total // lanes, some_blocks, 0)


def backproject(thick, seg_rows, tile_rows, order, starts, counts, tiles, first, blocks, capacity):
    angles, segments, rows, edge = thick[0].shape
    groups = starts.shape[0]
    smem = pl.BlockSpec(memory_space=pltpu.SMEM)
    vmem = pl.BlockSpec(memory_space=pltpu.VMEM)
    flops = 2 * len(thick) * angles * blocks * rows * edge * edge
    return pl.pallas_call(
        functools.partial(backproject_kernel, first),
        out_shape=jax.ShapeDtypeStruct((groups, blocks, capacity, edge), jnp.float32),
        in_specs=[smem] * 5 + [vmem] * (len(thick) + 1),
        out_specs=vmem,
        scratch_shapes=[pltpu.VMEM((unroll_blocks, rows + capacity, edge), jnp.float32)],
        compiler_params=pltpu.CompilerParams(vmem_limit_bytes=32 * 2**20),
        cost_estimate=pl.CostEstimate(
            flops=flops, bytes_accessed=4 * groups * blocks * capacity * edge, transcendentals=0
        ),
        name="backproject",
    )(seg_rows, tile_rows, order, starts, counts, *thick, tiles)


def butterfly(partial, scale, lead):
    total = partial.shape[0]
    bits = total.bit_length() - 1
    remaining = list(range(bits - 1, -1, -1))
    current = partial.reshape((2,) * bits + partial.shape[1:])
    order = list(range(bits))
    if bits > 1 and lead:
        order[0], order[1] = order[1], order[0]
    for bit in order:
        axis = remaining.index(bit)
        remaining.remove(bit)
        keep = lax.index_in_dim(current, 0, axis, keepdims=False)
        send = lax.index_in_dim(current, 1, axis, keepdims=False)
        pairs = [(i, i ^ (1 << bit)) for i in range(total)]
        came = lax.ppermute((send * scale).astype(link_type), "angle", pairs)
        current = keep + came.astype(jnp.float32) / scale
    return current


def per_device(intensity, counts, segment_ids, tile_ids, block_order, tiles):
    angles, rows, _ = intensity.shape
    edge = tiles.shape[1]
    groups = lax.axis_size("angle")
    cores = lax.axis_size("tile")
    place = lax.axis_index("angle")
    core = lax.axis_index("tile")
    capacity = 2 * rows // groups
    blocks = block_order.shape[0] // cores
    angle_total = segment_ids.shape[0]

    thickness = paganin_thickness(intensity, edge)
    thick, angle_rows = [thickness], [(place * cores + core) * angles]
    for step in range(1, cores):
        pairs = [(i, (i + step) % cores) for i in range(cores)]
        thick.append(lax.ppermute(thickness, "tile", pairs))
        angle_rows.append((place * cores + (core - step) % cores) * angles)

    seg_rows = jnp.concatenate(
        [lax.dynamic_slice_in_dim(segment_ids, row, angles) for row in angle_rows]
    )
    tile_rows = jnp.concatenate(
        [lax.dynamic_slice_in_dim(tile_ids, row, angles) for row in angle_rows]
    )
    order = lax.dynamic_slice_in_dim(block_order, core * blocks, blocks)
    relative = jnp.arange(groups, dtype=jnp.int32)
    member = relative[None, :] == (relative ^ place)[:, None]
    before = relative[None, :] < (relative ^ place)[:, None]
    near_counts = jnp.sum(jnp.where(member, counts[None, :], 0), axis=1)
    near_starts = jnp.sum(jnp.where(before, counts[None, :], 0), axis=1)

    largest = jnp.max(jnp.abs(tiles.astype(jnp.float32)))
    bound = 1.75 * angle_total * edge * jnp.where(largest > 0.0, largest, 1.0)
    scale = 60000.0 / bound

    chunks = math.gcd(chunk_total, blocks)
    per_chunk = blocks // chunks
    finished = []
    for c in range(chunks):
        partial = backproject(
            thick, seg_rows, tile_rows, order, near_starts, near_counts, tiles,
            c * per_chunk, per_chunk, capacity,
        )
        finished.append(butterfly(partial, scale, c % 2))
    volume = jnp.concatenate(finished, axis=0)
    return jnp.swapaxes(volume, 0, 1)[None]


def solution(mesh):
    in_specs = (P(("groups", "angle", "tile"), None, None), P("groups"), P(), P(), P("groups"), P())
    out_specs = P(("groups", "angle"), None, "tile", None)
    return jax.shard_map(
        per_device, mesh=mesh, in_specs=in_specs, out_specs=out_specs, check_vma=False
    )
```

```python
import functools
import math

import jax
import jax.numpy as jnp
import numpy as np
from jax import lax
from jax.experimental import pallas as pl
from jax.experimental.pallas import tpu as pltpu
from jax.sharding import PartitionSpec as P

paganin_alpha = 2.0
chunk_total = 8
variant_every = 4
lag = 2
code_top = 32760.0
round_shift = 12582912.0
MESH = pl.DeviceIdType.MESH
pitch_extra = 9


def split_pair(array):
    high = array.astype(jnp.bfloat16)
    low = (array - high.astype(jnp.float32)).astype(jnp.bfloat16)
    return high, low


def filter_tables(row_total, edge):
    index = np.arange(row_total)
    phase = 2.0 * np.pi * (index[:, None] * index[None, :] % row_total) / row_total
    hartley = (np.cos(phase) + np.sin(phase)) / math.sqrt(row_total)
    a = 1.0 + paganin_alpha * (4.0 * np.sin(np.pi * index / row_total) ** 2 + 2.0)
    pole = (a - np.sqrt(a * a - 4.0 * paganin_alpha**2)) / (2.0 * paganin_alpha)
    gain = pole / (paganin_alpha * (1.0 - pole * pole))

    def halves(matrix):
        high = matrix.astype(np.float32).astype(jnp.bfloat16)
        return high, (matrix - high.astype(np.float64)).astype(np.float32).astype(jnp.bfloat16)

    high, low = halves(hartley * gain[None, :])
    forward = np.concatenate([np.concatenate([high, low], 1)] * 2, 0)
    high, low = halves(hartley)
    inverse = np.concatenate([np.concatenate([high, high], 1), np.concatenate([low, low], 1)], 0)
    reach = pole[None, :] ** np.arange(1, edge + 1)[:, None]
    powers = np.concatenate([reach, reach[::-1]], 0).astype(np.float32)
    return forward, inverse, powers


def filter_kernel(x_ref, forward_ref, inverse_ref, power_ref, out_ref, spectrum, ahead_ref, behind_ref, ends):
    edge = out_ref.shape[-1]
    segments = out_ref.shape[1]
    rows = out_ref.shape[2]
    pitch = edge + pitch_extra
    for s in range(segments):
        high, low = split_pair(x_ref[0, :, s * edge : (s + 1) * edge])
        both = jnp.concatenate([high, low], axis=0)
        product = lax.dot_general(
            both, forward_ref[...], (((0,), (0,)), ((), ())), preferred_element_type=jnp.float32
        )
        spectrum[s * pitch : s * pitch + edge, :] = product[:, :rows] + product[:, rows:]
    pole = jnp.broadcast_to(power_ref[0:1, :], (segments, rows))
    zero = jnp.zeros((segments, rows), jnp.float32)

    def column(t):
        return pl.ds(t, segments, stride=pitch)

    def sweep(t, state):
        ahead, behind = state
        ahead = ahead * pole + spectrum[column(t), :]
        ahead_ref[column(t), :] = ahead
        back = edge - 1 - t
        behind = behind * pole
        behind_ref[column(back), :] = behind
        return ahead, behind + spectrum[column(back), :]

    ahead, behind = lax.fori_loop(0, edge, sweep, (zero, zero), unroll=16)
    ends[0] = ahead
    ends[1] = behind
    for s in range(segments):
        span = slice(s * pitch, s * pitch + edge)
        before, after = (s - 1) % segments, (s + 1) % segments
        value = ahead_ref[span, :] + behind_ref[span, :]
        value = value + power_ref[:edge, :] * ends[0, before : before + 1, :]
        value = value + power_ref[edge:, :] * ends[1, after : after + 1, :]
        high, low = split_pair(value)
        both = jnp.concatenate([high, low], axis=1)
        product = lax.dot_general(
            inverse_ref[...], both, (((1,), (1,)), ((), ())), preferred_element_type=jnp.float32
        )
        out_ref[0, s] = (-jnp.log(product[:rows] + product[rows:])).astype(jnp.bfloat16)


def paganin_thickness(intensity, edge):
    angles, rows, width = intensity.shape
    forward, inverse, powers = filter_tables(rows, edge)
    segments = width // edge
    whole = lambda *shape: pl.BlockSpec(shape, lambda a: (0,) * len(shape))
    plane = pltpu.VMEM((segments * (edge + pitch_extra), rows), jnp.float32)
    return pl.pallas_call(
        filter_kernel,
        grid=(angles,),
        out_shape=jax.ShapeDtypeStruct((angles, segments, rows, edge), jnp.bfloat16),
        in_specs=[
            pl.BlockSpec((1, rows, width), lambda a: (a, 0, 0)),
            whole(2 * rows, 2 * rows),
            whole(2 * rows, 2 * rows),
            whole(2 * edge, rows),
        ],
        out_specs=pl.BlockSpec((1, segments, rows, edge), lambda a: (a, 0, 0, 0)),
        scratch_shapes=[plane, plane, plane, pltpu.VMEM((2, segments, rows), jnp.float32)],
        compiler_params=pltpu.CompilerParams(vmem_limit_bytes=60 * 2**20),
        name="paganin_filter",
    )(intensity, jnp.asarray(forward), jnp.asarray(inverse), jnp.asarray(powers))


def encode(value):
    top = jnp.maximum(jnp.max(jnp.abs(value), axis=0, keepdims=True), 1e-30)
    scaled = value * (code_top / top)
    code = (scaled + round_shift) - round_shift
    return code.astype(jnp.int32).astype(jnp.int16), top * (1.0 / code_top)


def decode(code, unit):
    return code.astype(jnp.int32).astype(jnp.float32) * unit


def reduce_kernel(
    stages, cores, chunks, seg_ref, tile_ref, order_ref, start_ref, count_ref, own, tiles_ref, out_ref,
    other, rows_ref, part, kept, swap_send, swap_recv, data_send, data_recv, unit_send, unit_recv, *buffers
):
    send, came, send_unit, came_unit = (buffers[i * stages : (i + 1) * stages] for i in range(4))
    groups = 2**stages
    angles, _, rows, edge = own.shape
    blocks, capacity, _ = out_ref.shape
    per_chunk = blocks // chunks
    place, core = lax.axis_index("angle"), lax.axis_index("tile")

    def across(bit):
        return place + (1 - 2 * ((place // (1 << bit)) % 2)) * (1 << bit)

    partners = [across(bit) for bit in range(stages)]
    neighbours = [lax.rem(core + step, cores) for step in range(1, cores)]
    barrier = pltpu.get_barrier_semaphore()
    for partner in partners:
        pl.semaphore_signal(barrier, inc=1, device_id={"angle": partner}, device_id_type=MESH)
    for neighbour in neighbours:
        pl.semaphore_signal(barrier, inc=1, device_id={"tile": neighbour}, device_id_type=MESH)
    pl.semaphore_wait(barrier, stages + cores - 1)

    swaps = []
    for index, neighbour in enumerate(neighbours):
        for a in range(angles):
            swaps.append(
                pltpu.make_async_remote_copy(
                    src_ref=own.at[a],
                    dst_ref=other.at[index, a],
                    send_sem=swap_send.at[index, a],
                    recv_sem=swap_recv.at[index, a],
                    device_id={"tile": neighbour},
                    device_id_type=MESH,
                )
            )
            swaps[-1].start()

    for lane in range(per_chunk):
        rows_ref[lane, rows:, :] = jnp.zeros((capacity, edge), jnp.float32)
    slot = lax.broadcasted_iota(jnp.int32, (capacity, edge), 0)

    def project(sources, first_row, block):
        pieces, maps = [], []
        for index, thick in enumerate(sources):
            for a in range(angles):
                row = first_row + index * angles + a
                pieces.append(thick(a, seg_ref[row, block]))
                maps.append(tiles_ref[tile_ref[row, block]])
        return jnp.dot(
            jnp.concatenate(pieces, axis=1),
            jnp.concatenate(maps, axis=0),
            preferred_element_type=jnp.float32,
        )

    def own_part(step, _):
        for lane in range(per_chunk):
            v = step * per_chunk + lane
            part[v] = project([lambda a, s: own[a, s]], 0, order_ref[v])
        return 0

    lax.fori_loop(0, chunks, own_part, 0)
    for swap in swaps:
        swap.wait()
    others = [lambda a, s, index=index: other[index, a, s] for index in range(cores - 1)]

    def variant_of(c):
        return (c % variant_every) // (variant_every - 1) if stages > 1 else 0

    def copies(stage, c):
        partner = partners[stage]
        if stages > 1 and stage < 2:
            variant = variant_of(c)
            partner = partners[stage] * (1 - variant) + partners[1 - stage] * variant
        made = []
        for source, target, sent, got in (
            (send[stage], came[stage], data_send, data_recv),
            (send_unit[stage], came_unit[stage], unit_send, unit_recv),
        ):
            made.append(
                pltpu.make_async_remote_copy(
                    src_ref=source.at[c],
                    dst_ref=target.at[c],
                    send_sem=sent.at[stage, c],
                    recv_sem=got.at[stage, c],
                    device_id={"angle": partner},
                    device_id_type=MESH,
                )
            )
        return made

    def ship(stage, c, lane, position, value):
        half = groups >> (stage + 1)
        code, unit = encode(value)
        send[stage][c, lane, position - half] = code
        send_unit[stage][c, lane * half + position - half : lane * half + position - half + 1, :] = unit

    def begin(c):
        variant = variant_of(c)
        for lane in range(per_chunk):
            v = c * per_chunk + lane
            rows_ref[lane, :rows, :] = part[v] + project(others, angles, order_ref[v])
        for lane in range(per_chunk):
            v = c * per_chunk + lane
            for g in range(groups):
                picked = rows_ref[lane, pl.ds(start_ref[variant, g], capacity), :]
                picked = jnp.where(slot < count_ref[variant, g], picked, 0.0)
                if g < groups // 2:
                    kept[v, g] = picked
                else:
                    ship(0, c, lane, g, picked)
        for copy in copies(0, c):
            copy.start()

    def advance(stage, c):
        for copy in copies(stage - 1, c):
            copy.wait()
        left = groups >> stage
        for lane in range(per_chunk):
            v = c * per_chunk + lane
            for g in range(left):
                unit = came_unit[stage - 1][c, lane * left + g : lane * left + g + 1, :]
                value = kept[v, g] + decode(came[stage - 1][c, lane, g], unit)
                if stage == stages:
                    out_ref[v] = value
                elif g < left // 2:
                    kept[v, g] = value
                else:
                    ship(stage, c, lane, g, value)
        if stage < stages:
            for copy in copies(stage, c):
                copy.start()

    def step_body(step, _):
        @pl.when(step < chunks)
        def _():
            begin(step)

        for stage in range(stages, 0, -1):
            c = step - stage * lag

            @pl.when((c >= 0) & (c < chunks))
            def _(stage=stage, c=c):
                advance(stage, c)

        return 0

    lax.fori_loop(0, chunks + stages * lag, step_body, 0)


def reduced_blocks(thickness, seg_rows, tile_rows, order, starts, counts, tiles, capacity, cores):
    angles, segments, rows, edge = thickness.shape
    groups = starts.shape[1]
    stages = groups.bit_length() - 1
    blocks = order.shape[0]
    chunks = math.gcd(chunk_total, blocks)
    per_chunk = blocks // chunks
    smem = pl.BlockSpec(memory_space=pltpu.SMEM)
    vmem = pl.BlockSpec(memory_space=pltpu.VMEM)
    dma = pltpu.SemaphoreType.DMA
    halves = [groups >> (stage + 1) for stage in range(stages)]
    data = [pltpu.VMEM((chunks, per_chunk, half, capacity, edge), jnp.int16) for half in halves]
    unit = [pltpu.VMEM((chunks, per_chunk * half, edge), jnp.float32) for half in halves]
    return pl.pallas_call(
        functools.partial(reduce_kernel, stages, cores, chunks),
        out_shape=jax.ShapeDtypeStruct((blocks, capacity, edge), jnp.float32),
        in_specs=[smem] * 5 + [vmem] * 2,
        out_specs=vmem,
        scratch_shapes=[
            pltpu.VMEM((cores - 1, angles, segments, rows, edge), jnp.bfloat16),
            pltpu.VMEM((per_chunk, rows + capacity, edge), jnp.float32),
            pltpu.VMEM((blocks, rows, edge), jnp.float32),
            pltpu.VMEM((blocks, groups // 2, capacity, edge), jnp.float32),
            dma((cores - 1, angles)),
            dma((cores - 1, angles)),
            dma((stages, chunks)),
            dma((stages, chunks)),
            dma((stages, chunks)),
            dma((stages, chunks)),
            *data, *data, *unit, *unit,
        ],
        compiler_params=pltpu.CompilerParams(
            vmem_limit_bytes=40 * 2**20, collective_id=0, has_side_effects=True
        ),
        name="backproject_reduce",
    )(seg_rows, tile_rows, order, starts, counts, thickness, tiles)


def per_device(intensity, counts, segment_ids, tile_ids, block_order, tiles):
    angles, rows, _ = intensity.shape
    edge = tiles.shape[1]
    groups = lax.axis_size("angle")
    cores = lax.axis_size("tile")
    place = lax.axis_index("angle")
    core = lax.axis_index("tile")
    capacity = 2 * rows // groups
    blocks = block_order.shape[0] // cores

    thickness = paganin_thickness(intensity, edge)
    angle_rows = [
        (place * cores + (core - step) % cores) * angles for step in range(cores)
    ]
    seg_rows = jnp.concatenate(
        [lax.dynamic_slice_in_dim(segment_ids, row, angles) for row in angle_rows]
    )
    tile_rows = jnp.concatenate(
        [lax.dynamic_slice_in_dim(tile_ids, row, angles) for row in angle_rows]
    )
    order = lax.dynamic_slice_in_dim(block_order, core * blocks, blocks)

    stages = groups.bit_length() - 1
    bit_order = list(range(stages))
    swapped = bit_order[:]
    if stages > 1:
        swapped[0], swapped[1] = 1, 0
    offsets = np.array(
        [
            [sum(((p >> (stages - 1 - i)) & 1) << bits[i] for i in range(stages)) for p in range(groups)]
            for bits in (bit_order, swapped)
        ],
        np.int32,
    )
    owner = jnp.asarray(offsets) ^ place
    index = jnp.arange(groups, dtype=jnp.int32)
    near_counts = jnp.sum(jnp.where(index == owner[..., None], counts, 0), axis=-1)
    near_starts = jnp.sum(jnp.where(index < owner[..., None], counts, 0), axis=-1)
    volume = reduced_blocks(
        thickness, seg_rows, tile_rows, order, near_starts, near_counts, tiles, capacity, cores
    )
    return jnp.swapaxes(volume, 0, 1)[None]


def solution(mesh):
    in_specs = (P(("groups", "angle", "tile"), None, None), P("groups"), P(), P(), P("groups"), P())
    out_specs = P(("groups", "angle"), None, "tile", None)
    return jax.shard_map(
        per_device, mesh=mesh, in_specs=in_specs, out_specs=out_specs, check_vma=False
    )
```

```python
import functools
import math

import jax
import jax.numpy as jnp
import numpy as np
from jax import lax
from jax.experimental import pallas as pl
from jax.experimental.pallas import tpu as pltpu
from jax.sharding import PartitionSpec as P

paganin_alpha = 2.0
chunk_total = 16
lag = 3
code_top = 32760.0
round_shift = 12582912.0
MESH = pl.DeviceIdType.MESH
pitch_extra = 9


def split_pair(array):
    high = array.astype(jnp.bfloat16)
    low = (array - high.astype(jnp.float32)).astype(jnp.bfloat16)
    return high, low


def filter_tables(row_total, edge):
    index = np.arange(row_total)
    phase = 2.0 * np.pi * (index[:, None] * index[None, :] % row_total) / row_total
    hartley = (np.cos(phase) + np.sin(phase)) / math.sqrt(row_total)
    a = 1.0 + paganin_alpha * (4.0 * np.sin(np.pi * index / row_total) ** 2 + 2.0)
    pole = (a - np.sqrt(a * a - 4.0 * paganin_alpha**2)) / (2.0 * paganin_alpha)
    gain = pole / (paganin_alpha * (1.0 - pole * pole))

    def halves(matrix):
        high = matrix.astype(np.float32).astype(jnp.bfloat16)
        return high, (matrix - high.astype(np.float64)).astype(np.float32).astype(jnp.bfloat16)

    high, low = halves(hartley * gain[None, :])
    forward = np.concatenate([np.concatenate([high, low], 1)] * 2, 0)
    high, low = halves(hartley)
    inverse = np.concatenate([np.concatenate([high, high], 1), np.concatenate([low, low], 1)], 0)
    reach = pole[None, :] ** np.arange(1, edge + 1)[:, None]
    powers = np.concatenate([reach, reach[::-1]], 0).astype(np.float32)
    return forward, inverse, powers


def filter_one(x_ref, forward_ref, inverse_ref, power_ref, out_ref, spectrum, ahead_ref, behind_ref, ends):
    segments, rows, edge = out_ref.shape
    pitch = edge + pitch_extra
    for s in range(segments):
        high, low = split_pair(x_ref[:, s * edge : (s + 1) * edge])
        both = jnp.concatenate([high, low], axis=0)
        product = lax.dot_general(
            both, forward_ref[...], (((0,), (0,)), ((), ())), preferred_element_type=jnp.float32
        )
        spectrum[s * pitch : s * pitch + edge, :] = product[:, :rows] + product[:, rows:]
    pole = jnp.broadcast_to(power_ref[0:1, :], (segments, rows))
    zero = jnp.zeros((segments, rows), jnp.float32)

    def column(t):
        return pl.ds(t, segments, stride=pitch)

    def sweep(t, state):
        ahead, behind = state
        ahead = ahead * pole + spectrum[column(t), :]
        ahead_ref[column(t), :] = ahead
        back = edge - 1 - t
        behind = behind * pole
        behind_ref[column(back), :] = behind
        return ahead, behind + spectrum[column(back), :]

    ahead, behind = lax.fori_loop(0, edge, sweep, (zero, zero), unroll=16)
    ends[0] = ahead
    ends[1] = behind
    for s in range(segments):
        span = slice(s * pitch, s * pitch + edge)
        before, after = (s - 1) % segments, (s + 1) % segments
        value = ahead_ref[span, :] + behind_ref[span, :]
        value = value + power_ref[:edge, :] * ends[0, before : before + 1, :]
        value = value + power_ref[edge:, :] * ends[1, after : after + 1, :]
        high, low = split_pair(value)
        both = jnp.concatenate([high, low], axis=1)
        product = lax.dot_general(
            inverse_ref[...], both, (((1,), (1,)), ((), ())), preferred_element_type=jnp.float32
        )
        out_ref[s] = (-jnp.log(product[:rows] + product[rows:])).astype(jnp.bfloat16)


def encode(value):
    top = jnp.maximum(jnp.max(jnp.abs(value), axis=0, keepdims=True), 1e-30)
    scaled = value * (code_top / top)
    code = (scaled + round_shift) - round_shift
    return code.astype(jnp.int32).astype(jnp.int16), top * (1.0 / code_top)


def decode(code, unit):
    return code.astype(jnp.int32).astype(jnp.float32) * unit


def whole_kernel(
    stages, cores, chunks, count_ref, seg_ref, tile_ref, order_ref, x_hbm, forward_hbm, inverse_hbm,
    power_hbm, tiles_hbm, out_ref, x_buf, forward_ref, inverse_ref, power_ref, tiles_ref, spectrum,
    ahead_ref, behind_ref, ends, own, other, start_ref, rows_ref, kept, x_sem, load_sem, swap_send,
    swap_recv, data_send, data_recv, unit_send, unit_recv, *buffers
):
    send, came, send_unit, came_unit = (buffers[i * stages : (i + 1) * stages] for i in range(4))
    groups = 2**stages
    angles, _, rows, edge = own.shape
    blocks, capacity, _ = out_ref.shape
    per_chunk = blocks // chunks
    place, core = lax.axis_index("angle"), lax.axis_index("tile")

    loads = [
        pltpu.make_async_copy(source, target, load_sem.at[i])
        for i, (source, target) in enumerate(
            (
                (forward_hbm, forward_ref),
                (power_hbm, power_ref),
                (inverse_hbm, inverse_ref),
                (tiles_hbm, tiles_ref),
            )
        )
    ]

    def projection(a):
        return pltpu.make_async_copy(x_hbm.at[a], x_buf.at[a], x_sem.at[a])

    projection(0).start()
    for load in loads[:3]:
        load.start()
    for a in range(1, angles):
        projection(a).start()
    loads[3].start()

    def across(bit):
        return place + (1 - 2 * ((place // (1 << bit)) % 2)) * (1 << bit)

    partners = [across(bit) for bit in range(stages)]
    neighbours = [lax.rem(core + step, cores) for step in range(1, cores)]
    barrier = pltpu.get_barrier_semaphore()
    for partner in partners:
        pl.semaphore_signal(barrier, inc=1, device_id={"angle": partner}, device_id_type=MESH)
    for neighbour in neighbours:
        pl.semaphore_signal(barrier, inc=1, device_id={"tile": neighbour}, device_id_type=MESH)

    running = jnp.int32(0)
    for g in range(groups):
        start_ref[g] = running
        running = running + count_ref[g]
    for lane in range(per_chunk):
        rows_ref[lane, rows:, :] = jnp.zeros((capacity, edge), jnp.float32)
    for load in loads[:3]:
        load.wait()

    def swap(index, a):
        return pltpu.make_async_remote_copy(
            src_ref=own.at[a],
            dst_ref=other.at[index, a],
            send_sem=swap_send.at[index, a],
            recv_sem=swap_recv.at[index, a],
            device_id={"tile": neighbours[index]},
            device_id_type=MESH,
        )

    def filter_angle(a, _):
        projection(a).wait()
        filter_one(
            x_buf.at[a], forward_ref, inverse_ref, power_ref, own.at[a],
            spectrum, ahead_ref, behind_ref, ends,
        )

        @pl.when(a == 0)
        def _():
            pl.semaphore_wait(barrier, stages + cores - 1)

        for index in range(cores - 1):
            swap(index, a).start()
        return 0

    lax.fori_loop(0, angles, filter_angle, 0)
    loads[3].wait()
    for index in range(cores - 1):
        for a in range(angles):
            swap(index, a).wait()

    slot = lax.broadcasted_iota(jnp.int32, (capacity, edge), 0)
    thick_rows = [(lambda a, s: own[a, s], (place * cores + core) * angles)]
    for index in range(cores - 1):
        source = lax.rem(core + cores - 1 - index, cores)
        thick_rows.append(
            (lambda a, s, index=index: other[index, a, s], (place * cores + source) * angles)
        )

    def project(v):
        block = order_ref[core * blocks + v]
        pieces, maps = [], []
        for thick, first_row in thick_rows:
            for a in range(angles):
                pieces.append(thick(a, seg_ref[first_row + a, block]))
                maps.append(tiles_ref[tile_ref[first_row + a, block]])
        return jnp.dot(
            jnp.concatenate(pieces, axis=1),
            jnp.concatenate(maps, axis=0),
            preferred_element_type=jnp.float32,
        )

    def variant_of(c):
        return ((c + 2) % 4) // 3 if stages > 1 else 0

    def owner(variant, position):
        group = place
        for i in range(stages):
            if (position >> (stages - 1 - i)) & 1:
                move = partners[i] - place
                if stages > 1 and i < 2:
                    move = move * (1 - variant) + (partners[1 - i] - place) * variant
                group = group + move
        return group

    def copies(stage, c):
        partner = partners[stage]
        if stages > 1 and stage < 2:
            variant = variant_of(c)
            partner = partners[stage] * (1 - variant) + partners[1 - stage] * variant
        made = []
        for source, target, sent, got in (
            (send[stage], came[stage], data_send, data_recv),
            (send_unit[stage], came_unit[stage], unit_send, unit_recv),
        ):
            made.append(
                pltpu.make_async_remote_copy(
                    src_ref=source.at[c],
                    dst_ref=target.at[c],
                    send_sem=sent.at[stage, c],
                    recv_sem=got.at[stage, c],
                    device_id={"angle": partner},
                    device_id_type=MESH,
                )
            )
        return made

    def ship(stage, c, lane, position, value):
        half = groups >> (stage + 1)
        code, unit = encode(value)
        send[stage][c, lane, position - half] = code
        send_unit[stage][c, lane * half + position - half : lane * half + position - half + 1, :] = unit

    def begin(c):
        variant = variant_of(c)
        for lane in range(per_chunk):
            v = c * per_chunk + lane
            rows_ref[lane, :rows, :] = project(v)
        for g in range(groups):
            group = owner(variant, g)
            start, count = start_ref[group], count_ref[group]
            for lane in range(per_chunk):
                v = c * per_chunk + lane
                picked = rows_ref[lane, pl.ds(start, capacity), :]
                picked = jnp.where(slot < count, picked, 0.0)
                if g < groups // 2:
                    kept[v, g] = picked
                else:
                    ship(0, c, lane, g, picked)
        for copy in copies(0, c):
            copy.start()

    def advance(stage, c):
        for copy in copies(stage - 1, c):
            copy.wait()
        left = groups >> stage
        for lane in range(per_chunk):
            v = c * per_chunk + lane
            for g in range(left):
                unit = came_unit[stage - 1][c, lane * left + g : lane * left + g + 1, :]
                value = kept[v, g] + decode(came[stage - 1][c, lane, g], unit)
                if stage == stages:
                    out_ref[v] = value
                elif g < left // 2:
                    kept[v, g] = value
                else:
                    ship(stage, c, lane, g, value)
        if stage < stages:
            for copy in copies(stage, c):
                copy.start()

    def step_body(step, _):
        @pl.when(step < chunks)
        def _():
            begin(step)

        for stage in range(stages, 0, -1):
            c = step - stage * lag

            @pl.when((c >= 0) & (c < chunks))
            def _(stage=stage, c=c):
                advance(stage, c)

        return 0

    lax.fori_loop(0, chunks + stages * lag, step_body, 0)


def per_device(intensity, counts, segment_ids, tile_ids, block_order, tiles):
    angles, rows, width = intensity.shape
    edge = tiles.shape[1]
    segments = width // edge
    groups = lax.axis_size("angle")
    cores = lax.axis_size("tile")
    stages = groups.bit_length() - 1
    capacity = 2 * rows // groups
    blocks = block_order.shape[0] // cores
    chunks = math.gcd(chunk_total, blocks)
    per_chunk = blocks // chunks
    forward, inverse, powers = filter_tables(rows, edge)

    smem = pl.BlockSpec(memory_space=pltpu.SMEM)
    vmem = pl.BlockSpec(memory_space=pltpu.VMEM)
    hbm = pl.BlockSpec(memory_space=pl.ANY)
    dma = pltpu.SemaphoreType.DMA
    f32, bf16 = jnp.float32, jnp.bfloat16
    plane = pltpu.VMEM((segments * (edge + pitch_extra), rows), f32)
    halves = [groups >> (stage + 1) for stage in range(stages)]
    data = [pltpu.VMEM((chunks, per_chunk, half, capacity, edge), jnp.int16) for half in halves]
    unit = [pltpu.VMEM((chunks, per_chunk * half, edge), f32) for half in halves]
    volume = pl.pallas_call(
        functools.partial(whole_kernel, stages, cores, chunks),
        out_shape=jax.ShapeDtypeStruct((blocks, capacity, edge), f32),
        in_specs=[smem] * 4 + [hbm] * 5,
        out_specs=vmem,
        scratch_shapes=[
            pltpu.VMEM(intensity.shape, f32),
            pltpu.VMEM(forward.shape, bf16),
            pltpu.VMEM(inverse.shape, bf16),
            pltpu.VMEM(powers.shape, f32),
            pltpu.VMEM(tiles.shape, bf16),
            plane, plane, plane,
            pltpu.VMEM((2, segments, rows), f32),
            pltpu.VMEM((angles, segments, rows, edge), bf16),
            pltpu.VMEM((cores - 1, angles, segments, rows, edge), bf16),
            pltpu.SMEM((groups,), jnp.int32),
            pltpu.VMEM((per_chunk, rows + capacity, edge), f32),
            pltpu.VMEM((blocks, groups // 2, capacity, edge), f32),
            dma((angles,)),
            dma((4,)),
            dma((cores - 1, angles)),
            dma((cores - 1, angles)),
            dma((stages, chunks)),
            dma((stages, chunks)),
            dma((stages, chunks)),
            dma((stages, chunks)),
            *data, *data, *unit, *unit,
        ],
        compiler_params=pltpu.CompilerParams(
            vmem_limit_bytes=60 * 2**20, collective_id=0, has_side_effects=True
        ),
        name="tomography",
    )(
        counts, segment_ids, tile_ids, block_order, intensity,
        jnp.asarray(forward), jnp.asarray(inverse), jnp.asarray(powers), tiles,
    )
    return jnp.swapaxes(volume, 0, 1)[None]


def solution(mesh):
    in_specs = (P(("groups", "angle", "tile"), None, None), P("groups"), P(), P(), P("groups"), P())
    out_specs = P(("groups", "angle"), None, "tile", None)
    return jax.shard_map(
        per_device, mesh=mesh, in_specs=in_specs, out_specs=out_specs, check_vma=False
    )
```

```python
import functools
import math

import jax
import jax.numpy as jnp
import numpy as np
from jax import lax
from jax.experimental import pallas as pl
from jax.experimental.pallas import tpu as pltpu
from jax.sharding import PartitionSpec as P

paganin_alpha = 2.0
chunk_total = 8
sublanes = 8
lag = 3
code_top = 32760.0
round_shift = 12582912.0
MESH = pl.DeviceIdType.MESH
pitch_extra = 9


def split_pair(array):
    high = array.astype(jnp.bfloat16)
    low = (array - high.astype(jnp.float32)).astype(jnp.bfloat16)
    return high, low


def filter_tables(row_total, edge):
    index = np.arange(row_total)
    phase = 2.0 * np.pi * (index[:, None] * index[None, :] % row_total) / row_total
    hartley = (np.cos(phase) + np.sin(phase)) / math.sqrt(row_total)
    a = 1.0 + paganin_alpha * (4.0 * np.sin(np.pi * index / row_total) ** 2 + 2.0)
    pole = (a - np.sqrt(a * a - 4.0 * paganin_alpha**2)) / (2.0 * paganin_alpha)
    gain = pole / (paganin_alpha * (1.0 - pole * pole))

    def halves(matrix):
        high = matrix.astype(np.float32).astype(jnp.bfloat16)
        return high, (matrix - high.astype(np.float64)).astype(np.float32).astype(jnp.bfloat16)

    high, low = halves(hartley * gain[None, :])
    forward = np.concatenate([np.concatenate([high, low], 1)] * 2, 0)
    high, low = halves(hartley)
    inverse = np.concatenate([np.concatenate([high, high], 1), np.concatenate([low, low], 1)], 0)
    reach = pole[None, :] ** np.arange(1, edge + 1)[:, None]
    powers = np.concatenate([reach, reach[::-1]], 0).astype(np.float32)
    return forward, inverse, powers


def filter_one(x_ref, forward_ref, inverse_ref, power_ref, out_ref, spectrum, ahead_ref, behind_ref, ends):
    segments, rows, edge = out_ref.shape
    pitch = edge + pitch_extra
    for s in range(segments):
        high, low = split_pair(x_ref[:, s * edge : (s + 1) * edge])
        both = jnp.concatenate([high, low], axis=0)
        product = lax.dot_general(
            both, forward_ref[...], (((0,), (0,)), ((), ())), preferred_element_type=jnp.float32
        )
        spectrum[s * pitch : s * pitch + edge, :] = product[:, :rows] + product[:, rows:]
    pole = jnp.broadcast_to(power_ref[0:1, :], (segments, rows))
    zero = jnp.zeros((segments, rows), jnp.float32)

    def column(t):
        return pl.ds(t, segments, stride=pitch)

    def sweep(t, state):
        ahead, behind = state
        ahead = ahead * pole + spectrum[column(t), :]
        ahead_ref[column(t), :] = ahead
        back = edge - 1 - t
        behind = behind * pole
        behind_ref[column(back), :] = behind
        return ahead, behind + spectrum[column(back), :]

    ahead, behind = lax.fori_loop(0, edge, sweep, (zero, zero), unroll=16)
    ends[0] = ahead
    ends[1] = behind
    for s in range(segments):
        span = slice(s * pitch, s * pitch + edge)
        before, after = (s - 1) % segments, (s + 1) % segments
        value = ahead_ref[span, :] + behind_ref[span, :]
        value = value + power_ref[:edge, :] * ends[0, before : before + 1, :]
        value = value + power_ref[edge:, :] * ends[1, after : after + 1, :]
        high, low = split_pair(value)
        both = jnp.concatenate([high, low], axis=1)
        product = lax.dot_general(
            inverse_ref[...], both, (((1,), (1,)), ((), ())), preferred_element_type=jnp.float32
        )
        out_ref[s] = (-jnp.log(product[:rows] + product[rows:])).astype(jnp.bfloat16)


def encode(value):
    top = jnp.maximum(jnp.max(jnp.abs(value), axis=0, keepdims=True), 1e-30)
    scaled = value * (code_top / top)
    code = (scaled + round_shift) - round_shift
    return code.astype(jnp.int32).astype(jnp.int16), top * (1.0 / code_top)


def decode(code, unit):
    return code.astype(jnp.int32).astype(jnp.float32) * unit


def whole_kernel(
    stages, cores, chunks, count_ref, seg_ref, tile_ref, order_ref, x_hbm, forward_hbm, inverse_hbm,
    power_hbm, tiles_hbm, out_ref, x_buf, forward_ref, inverse_ref, power_ref, tiles_ref, spectrum,
    ahead_ref, behind_ref, ends, own, other, start_ref, rows_ref, kept, x_sem, load_sem, swap_send,
    swap_recv, data_send, data_recv, unit_send, unit_recv, *buffers
):
    send, came, send_unit, came_unit = (buffers[i * stages : (i + 1) * stages] for i in range(4))
    groups = 2**stages
    angles, _, rows, edge = own.shape
    capacity, blocks, _ = out_ref.shape
    per_chunk = blocks // chunks
    place, core = lax.axis_index("angle"), lax.axis_index("tile")

    loads = [
        pltpu.make_async_copy(source, target, load_sem.at[i])
        for i, (source, target) in enumerate(
            (
                (forward_hbm, forward_ref),
                (power_hbm, power_ref),
                (inverse_hbm, inverse_ref),
                (tiles_hbm, tiles_ref),
            )
        )
    ]

    def projection(a):
        return pltpu.make_async_copy(x_hbm.at[a], x_buf.at[a], x_sem.at[a])

    projection(0).start()
    for load in loads[:3]:
        load.start()
    for a in range(1, angles):
        projection(a).start()
    loads[3].start()

    def across(bit):
        return place + (1 - 2 * ((place // (1 << bit)) % 2)) * (1 << bit)

    partners = [across(bit) for bit in range(stages)]
    neighbours = [lax.rem(core + step, cores) for step in range(1, cores)]
    barrier = pltpu.get_barrier_semaphore()
    for partner in partners:
        pl.semaphore_signal(barrier, inc=1, device_id={"angle": partner}, device_id_type=MESH)
    for neighbour in neighbours:
        pl.semaphore_signal(barrier, inc=1, device_id={"tile": neighbour}, device_id_type=MESH)

    running = jnp.int32(0)
    for g in range(groups):
        start_ref[g] = running
        running = running + count_ref[g]
    for lane in range(per_chunk):
        rows_ref[lane, rows:, :] = jnp.zeros((capacity, edge), jnp.float32)
    for load in loads[:3]:
        load.wait()

    def swap(index, a):
        return pltpu.make_async_remote_copy(
            src_ref=own.at[a],
            dst_ref=other.at[index, a],
            send_sem=swap_send.at[index, a],
            recv_sem=swap_recv.at[index, a],
            device_id={"tile": neighbours[index]},
            device_id_type=MESH,
        )

    def filter_angle(a, _):
        projection(a).wait()
        filter_one(
            x_buf.at[a], forward_ref, inverse_ref, power_ref, own.at[a],
            spectrum, ahead_ref, behind_ref, ends,
        )

        @pl.when(a == 0)
        def _():
            pl.semaphore_wait(barrier, stages + cores - 1)

        for index in range(cores - 1):
            swap(index, a).start()
        return 0

    lax.fori_loop(0, angles, filter_angle, 0)
    loads[3].wait()
    for index in range(cores - 1):
        for a in range(angles):
            swap(index, a).wait()

    slot = lax.broadcasted_iota(jnp.int32, (capacity, edge), 0)
    thick_rows = [(lambda a, s: own[a, s], (place * cores + core) * angles)]
    for index in range(cores - 1):
        source = lax.rem(core + cores - 1 - index, cores)
        thick_rows.append(
            (lambda a, s, index=index: other[index, a, s], (place * cores + source) * angles)
        )

    def project(v):
        block = order_ref[core * blocks + v]
        pieces, maps = [], []
        for thick, first_row in thick_rows:
            for a in range(angles):
                pieces.append(thick(a, seg_ref[first_row + a, block]))
                maps.append(tiles_ref[tile_ref[first_row + a, block]])
        return jnp.dot(
            jnp.concatenate(pieces, axis=1),
            jnp.concatenate(maps, axis=0),
            preferred_element_type=jnp.float32,
        )

    def variant_of(c):
        return (c + 1) % 2 if stages > 1 else 0

    def owner(variant, position):
        group = place
        for i in range(stages):
            if (position >> (stages - 1 - i)) & 1:
                move = partners[i] - place
                if stages > 1 and i < 2:
                    move = move * (1 - variant) + (partners[1 - i] - place) * variant
                group = group + move
        return group

    def copies(stage, c):
        partner = partners[stage]
        if stages > 1 and stage < 2:
            variant = variant_of(c)
            partner = partners[stage] * (1 - variant) + partners[1 - stage] * variant
        made = []
        for source, target, sent, got in (
            (send[stage], came[stage], data_send, data_recv),
            (send_unit[stage], came_unit[stage], unit_send, unit_recv),
        ):
            made.append(
                pltpu.make_async_remote_copy(
                    src_ref=source.at[c],
                    dst_ref=target.at[c],
                    send_sem=sent.at[stage, c],
                    recv_sem=got.at[stage, c],
                    device_id={"angle": partner},
                    device_id_type=MESH,
                )
            )
        return made

    def ship(stage, c, tiles_out):
        half = groups >> (stage + 1)
        coded = [(lane, g, *encode(value)) for lane, g, value in tiles_out]
        for lane, g, code, unit in coded:
            row = lane * half + g - half
            send[stage][c, lane, g - half] = code
            send_unit[stage][c, row : row + 1, :] = unit

    def begin(c):
        variant = variant_of(c)
        for lane in range(per_chunk):
            rows_ref[lane, :rows, :] = project(c * per_chunk + lane)
        spans = [owner(variant, g) for g in range(groups)]
        spans = [(start_ref[group], slot < count_ref[group]) for group in spans]

        def picked(lane, g):
            start, inside = spans[g]
            return jnp.where(inside, rows_ref[lane, pl.ds(start, capacity), :], 0.0)

        for lane in range(per_chunk):
            ship(0, c, [(lane, g, picked(lane, g)) for g in range(groups // 2, groups)])
        for copy in copies(0, c):
            copy.start()
        for lane in range(per_chunk):
            held = [picked(lane, g) for g in range(groups // 2)]
            for g, value in enumerate(held):
                kept[c * per_chunk + lane, g] = value

    def advance(stage, c):
        for copy in copies(stage - 1, c):
            copy.wait()
        left = groups >> stage

        def value(lane, g):
            unit = came_unit[stage - 1][c, lane * left + g : lane * left + g + 1, :]
            return kept[c * per_chunk + lane, g] + decode(came[stage - 1][c, lane, g], unit)

        if stage == stages:
            for lane, last in enumerate([value(lane, 0) for lane in range(per_chunk)]):
                kept[c * per_chunk + lane, 0] = last
            return
        half = left // 2
        lanes_at_once = max(1, 4 // half)
        for first in range(0, per_chunk, lanes_at_once):
            lanes = range(first, min(per_chunk, first + lanes_at_once))
            ship(stage, c, [(lane, g, value(lane, g)) for lane in lanes for g in range(half, left)])
        for copy in copies(stage, c):
            copy.start()
        for first in range(0, per_chunk, lanes_at_once):
            lanes = range(first, min(per_chunk, first + lanes_at_once))
            held = [(lane, g, value(lane, g)) for lane in lanes for g in range(half)]
            for lane, g, tile in held:
                kept[c * per_chunk + lane, g] = tile

    def step_body(step, _):
        @pl.when(step < chunks)
        def _():
            begin(step)

        for stage in range(stages, 0, -1):
            c = step - stage * lag

            @pl.when((c >= 0) & (c < chunks))
            def _(stage=stage, c=c):
                advance(stage, c)

        return 0

    lax.fori_loop(0, chunks + stages * lag, step_body, 0)
    for v in range(0, blocks, sublanes):
        out_ref[:, v : v + sublanes, :] = jnp.swapaxes(kept[v : v + sublanes, 0], 0, 1)


def per_device(intensity, counts, segment_ids, tile_ids, block_order, tiles):
    angles, rows, width = intensity.shape
    edge = tiles.shape[1]
    segments = width // edge
    groups = lax.axis_size("angle")
    cores = lax.axis_size("tile")
    stages = groups.bit_length() - 1
    capacity = 2 * rows // groups
    blocks = block_order.shape[0] // cores
    chunks = math.gcd(chunk_total, blocks)
    per_chunk = blocks // chunks
    forward, inverse, powers = filter_tables(rows, edge)

    smem = pl.BlockSpec(memory_space=pltpu.SMEM)
    vmem = pl.BlockSpec(memory_space=pltpu.VMEM)
    hbm = pl.BlockSpec(memory_space=pl.ANY)
    dma = pltpu.SemaphoreType.DMA
    f32, bf16 = jnp.float32, jnp.bfloat16
    plane = pltpu.VMEM((segments * (edge + pitch_extra), rows), f32)
    halves = [groups >> (stage + 1) for stage in range(stages)]
    data = [pltpu.VMEM((chunks, per_chunk, half, capacity, edge), jnp.int16) for half in halves]
    unit = [pltpu.VMEM((chunks, per_chunk * half, edge), f32) for half in halves]
    volume = pl.pallas_call(
        functools.partial(whole_kernel, stages, cores, chunks),
        out_shape=jax.ShapeDtypeStruct((capacity, blocks, edge), f32),
        in_specs=[smem] * 4 + [hbm] * 5,
        out_specs=vmem,
        scratch_shapes=[
            pltpu.VMEM(intensity.shape, f32),
            pltpu.VMEM(forward.shape, bf16),
            pltpu.VMEM(inverse.shape, bf16),
            pltpu.VMEM(powers.shape, f32),
            pltpu.VMEM(tiles.shape, bf16),
            plane, plane, plane,
            pltpu.VMEM((2, segments, rows), f32),
            pltpu.VMEM((angles, segments, rows, edge), bf16),
            pltpu.VMEM((cores - 1, angles, segments, rows, edge), bf16),
            pltpu.SMEM((groups,), jnp.int32),
            pltpu.VMEM((per_chunk, rows + capacity, edge), f32),
            pltpu.VMEM((blocks, groups // 2, capacity, edge), f32),
            dma((angles,)),
            dma((4,)),
            dma((cores - 1, angles)),
            dma((cores - 1, angles)),
            dma((stages, chunks)),
            dma((stages, chunks)),
            dma((stages, chunks)),
            dma((stages, chunks)),
            *data, *data, *unit, *unit,
        ],
        compiler_params=pltpu.CompilerParams(
            vmem_limit_bytes=60 * 2**20, collective_id=0, has_side_effects=True
        ),
        name="tomography",
    )(
        counts, segment_ids, tile_ids, block_order, intensity,
        jnp.asarray(forward), jnp.asarray(inverse), jnp.asarray(powers), tiles,
    )
    return volume[None]


def solution(mesh):
    in_specs = (P(("groups", "angle", "tile"), None, None), P("groups"), P(), P(), P("groups"), P())
    out_specs = P(("groups", "angle"), None, "tile", None)
    return jax.shard_map(
        per_device, mesh=mesh, in_specs=in_specs, out_specs=out_specs, check_vma=False
    )
```

```python
import functools
import math

import jax
import jax.numpy as jnp
import numpy as np
from jax import lax
from jax.experimental import pallas as pl
from jax.experimental.pallas import tpu as pltpu
from jax.sharding import PartitionSpec as P

paganin_alpha = 2.0
chunk_total = 16
sublanes = 8
lag = 4
code_top = 32760.0
round_shift = 12582912.0
MESH = pl.DeviceIdType.MESH
pitch_extra = 9


def split_pair(array):
    high = array.astype(jnp.bfloat16)
    low = (array - high.astype(jnp.float32)).astype(jnp.bfloat16)
    return high, low


def filter_tables(row_total, edge):
    index = np.arange(row_total)
    phase = 2.0 * np.pi * (index[:, None] * index[None, :] % row_total) / row_total
    hartley = (np.cos(phase) + np.sin(phase)) / math.sqrt(row_total)
    a = 1.0 + paganin_alpha * (4.0 * np.sin(np.pi * index / row_total) ** 2 + 2.0)
    pole = (a - np.sqrt(a * a - 4.0 * paganin_alpha**2)) / (2.0 * paganin_alpha)
    gain = pole / (paganin_alpha * (1.0 - pole * pole))

    def halves(matrix):
        high = matrix.astype(np.float32).astype(jnp.bfloat16)
        return high, (matrix - high.astype(np.float64)).astype(np.float32).astype(jnp.bfloat16)

    high, low = halves(hartley * gain[None, :])
    forward = np.concatenate([np.concatenate([high, low], 1)] * 2, 0)
    high, low = halves(hartley)
    inverse = np.concatenate([np.concatenate([high, high], 1), np.concatenate([low, low], 1)], 0)
    reach = pole[None, :] ** np.arange(1, edge + 1)[:, None]
    powers = np.concatenate([reach, reach[::-1]], 0).astype(np.float32)
    return forward, inverse, powers


def spread(x_ref, forward_ref, spectrum, segments):
    rows, width = x_ref.shape
    edge = width // segments
    pitch = edge + pitch_extra
    for s in range(segments):
        high, low = split_pair(x_ref[:, s * edge : (s + 1) * edge])
        both = jnp.concatenate([high, low], axis=0)
        product = lax.dot_general(
            both, forward_ref[...], (((0,), (0,)), ((), ())), preferred_element_type=jnp.float32
        )
        spectrum[s * pitch : s * pitch + edge, :] = product[:, :rows] + product[:, rows:]


def sweep_columns(power_ref, planes, ends, segments, edge):
    rows = power_ref.shape[1]
    pole = jnp.broadcast_to(power_ref[0:1, :], (segments, rows))
    zero = jnp.zeros((segments, rows), jnp.float32)

    def column(t):
        return pl.ds(t, segments, stride=edge + pitch_extra)

    def sweep(t, states):
        back = edge - 1 - t
        inputs = [
            (spectrum[column(t), :], spectrum[column(back), :]) for spectrum, _, _ in planes
        ]
        following = []
        for (_, ahead_ref, behind_ref), (x, y), (ahead, behind) in zip(planes, inputs, states):
            ahead = ahead * pole + x
            behind = behind * pole
            ahead_ref[column(t), :] = ahead
            behind_ref[column(back), :] = behind
            following.append((ahead, behind + y))
        return following

    states = lax.fori_loop(0, edge, sweep, [(zero, zero) for _ in planes], unroll=8)
    for k, (ahead, behind) in enumerate(states):
        ends[k, 0] = ahead
        ends[k, 1] = behind


def finish(inverse_ref, power_ref, ahead_ref, behind_ref, ends, out_ref):
    segments, rows, edge = out_ref.shape
    pitch = edge + pitch_extra
    for s in range(segments):
        span = slice(s * pitch, s * pitch + edge)
        before, after = (s - 1) % segments, (s + 1) % segments
        value = ahead_ref[span, :] + behind_ref[span, :]
        value = value + power_ref[:edge, :] * ends[0, before : before + 1, :]
        value = value + power_ref[edge:, :] * ends[1, after : after + 1, :]
        high, low = split_pair(value)
        both = jnp.concatenate([high, low], axis=1)
        product = lax.dot_general(
            inverse_ref[...], both, (((1,), (1,)), ((), ())), preferred_element_type=jnp.float32
        )
        out_ref[s] = (-jnp.log(product[:rows] + product[rows:])).astype(jnp.bfloat16)


def encode(value):
    top = jnp.maximum(jnp.max(jnp.abs(value), axis=0, keepdims=True), 1e-30)
    scaled = value * (code_top / top)
    code = (scaled + round_shift) - round_shift
    return code.astype(jnp.int32).astype(jnp.int16), top * (1.0 / code_top)


def decode(code, unit):
    return code.astype(jnp.int32).astype(jnp.float32) * unit


def whole_kernel(
    stages, cores, chunks, count_ref, seg_ref, tile_ref, order_ref, x_hbm, forward_hbm, inverse_hbm,
    power_hbm, tiles_hbm, out_ref, x_buf, forward_ref, inverse_ref, power_ref, tiles_ref, spectrum,
    ahead_ref, behind_ref, ends, own, other, start_ref, rows_ref, kept, x_sem, load_sem, swap_send,
    swap_recv, data_send, data_recv, unit_send, unit_recv, *buffers
):
    send, came, send_unit, came_unit = (buffers[i * stages : (i + 1) * stages] for i in range(4))
    groups = 2**stages
    angles, _, rows, edge = own.shape
    capacity, blocks, _ = out_ref.shape
    per_chunk = blocks // chunks
    together = spectrum.shape[0]
    place, core = lax.axis_index("angle"), lax.axis_index("tile")

    loads = [
        pltpu.make_async_copy(source, target, load_sem.at[i])
        for i, (source, target) in enumerate(
            (
                (forward_hbm, forward_ref),
                (power_hbm, power_ref),
                (inverse_hbm, inverse_ref),
                (tiles_hbm, tiles_ref),
            )
        )
    ]

    def projection(a):
        return pltpu.make_async_copy(x_hbm.at[a], x_buf.at[a], x_sem.at[a])

    projection(0).start()
    for load in loads[:3]:
        load.start()
    for a in range(1, angles):
        projection(a).start()
    loads[3].start()

    def across(bit):
        return place + (1 - 2 * ((place // (1 << bit)) % 2)) * (1 << bit)

    partners = [across(bit) for bit in range(stages)]
    neighbours = [lax.rem(core + step, cores) for step in range(1, cores)]
    barrier = pltpu.get_barrier_semaphore()
    for partner in partners:
        pl.semaphore_signal(barrier, inc=1, device_id={"angle": partner}, device_id_type=MESH)
    for neighbour in neighbours:
        pl.semaphore_signal(barrier, inc=1, device_id={"tile": neighbour}, device_id_type=MESH)

    running = jnp.int32(0)
    for g in range(groups):
        start_ref[g] = running
        running = running + count_ref[g]
    begin_chunks = rows_ref.shape[0] // per_chunk
    for lane in range(begin_chunks * per_chunk):
        rows_ref[lane, rows:, :] = jnp.zeros((capacity, edge), jnp.float32)
    for load in loads[:3]:
        load.wait()

    def swap(index, a):
        return pltpu.make_async_remote_copy(
            src_ref=own.at[a],
            dst_ref=other.at[index, a],
            send_sem=swap_send.at[index, a],
            recv_sem=swap_recv.at[index, a],
            device_id={"tile": neighbours[index]},
            device_id_type=MESH,
        )

    def filter_angles(step, _):
        planes = [(spectrum.at[k], ahead_ref.at[k], behind_ref.at[k]) for k in range(together)]
        for k in range(together):
            projection(step * together + k).wait()
            spread(x_buf.at[step * together + k], forward_ref, spectrum.at[k], own.shape[1])
        sweep_columns(power_ref, planes, ends, own.shape[1], edge)
        for k in range(together):
            a = step * together + k
            finish(inverse_ref, power_ref, ahead_ref.at[k], behind_ref.at[k], ends.at[k], own.at[a])
            if k == 0:

                @pl.when(step == 0)
                def _():
                    pl.semaphore_wait(barrier, stages + cores - 1)

            for index in range(cores - 1):
                swap(index, a).start()
        return 0

    lax.fori_loop(0, angles // together, filter_angles, 0)
    loads[3].wait()
    for index in range(cores - 1):
        for a in range(angles):
            swap(index, a).wait()

    slot = lax.broadcasted_iota(jnp.int32, (capacity, edge), 0)
    thick_rows = [(lambda a, s: own[a, s], (place * cores + core) * angles)]
    for index in range(cores - 1):
        source = lax.rem(core + cores - 1 - index, cores)
        thick_rows.append(
            (lambda a, s, index=index: other[index, a, s], (place * cores + source) * angles)
        )

    def project(v):
        block = order_ref[core * blocks + v]
        pieces, maps = [], []
        for thick, first_row in thick_rows:
            for a in range(angles):
                pieces.append(thick(a, seg_ref[first_row + a, block]))
                maps.append(tiles_ref[tile_ref[first_row + a, block]])
        return jnp.dot(
            jnp.concatenate(pieces, axis=1),
            jnp.concatenate(maps, axis=0),
            preferred_element_type=jnp.float32,
        )

    def variant_of(c):
        return (c + 1) % 2 if stages > 1 else 0

    def owner(variant, position):
        group = place
        for i in range(stages):
            if (position >> (stages - 1 - i)) & 1:
                move = partners[i] - place
                if stages > 1 and i < 2:
                    move = move * (1 - variant) + (partners[1 - i] - place) * variant
                group = group + move
        return group

    def copies(stage, c):
        partner = partners[stage]
        if stages > 1 and stage < 2:
            variant = variant_of(c)
            partner = partners[stage] * (1 - variant) + partners[1 - stage] * variant
        made = []
        for source, target, sent, got in (
            (send[stage], came[stage], data_send, data_recv),
            (send_unit[stage], came_unit[stage], unit_send, unit_recv),
        ):
            made.append(
                pltpu.make_async_remote_copy(
                    src_ref=source.at[c],
                    dst_ref=target.at[c],
                    send_sem=sent.at[stage, c],
                    recv_sem=got.at[stage, c],
                    device_id={"angle": partner},
                    device_id_type=MESH,
                )
            )
        return made

    def ship(stage, c, tiles_out):
        half = groups >> (stage + 1)
        coded = [(lane, g, *encode(value)) for lane, g, value in tiles_out]
        for lane, g, code, unit in coded:
            row = lane * half + g - half
            send[stage][c, lane, g - half] = code
            send_unit[stage][c, row : row + 1, :] = unit

    def begin(first):
        for lane in range(begin_chunks * per_chunk):
            rows_ref[lane, :rows, :] = project(first * per_chunk + lane)
        for k in range(begin_chunks):
            c = first + k
            spans = [owner(variant_of(c), g) for g in range(groups)]
            spans = [(start_ref[group], slot < count_ref[group]) for group in spans]

            def picked(lane, g):
                start, inside = spans[g]
                row = rows_ref[k * per_chunk + lane, pl.ds(start, capacity), :]
                return jnp.where(inside, row, 0.0)

            for lane in range(per_chunk):
                ship(0, c, [(lane, g, picked(lane, g)) for g in range(groups // 2, groups)])
            for copy in copies(0, c):
                copy.start()
            for lane in range(per_chunk):
                held = [picked(lane, g) for g in range(groups // 2)]
                for g, value in enumerate(held):
                    kept[c * per_chunk + lane, g] = value

    def advance(stage, c):
        for copy in copies(stage - 1, c):
            copy.wait()
        left = groups >> stage

        def value(lane, g):
            unit = came_unit[stage - 1][c, lane * left + g : lane * left + g + 1, :]
            return kept[c * per_chunk + lane, g] + decode(came[stage - 1][c, lane, g], unit)

        if stage == stages:
            for lane, last in enumerate([value(lane, 0) for lane in range(per_chunk)]):
                kept[c * per_chunk + lane, 0] = last
            return
        half = left // 2
        lanes_at_once = max(1, 4 // half)
        for first in range(0, per_chunk, lanes_at_once):
            lanes = range(first, min(per_chunk, first + lanes_at_once))
            ship(stage, c, [(lane, g, value(lane, g)) for lane in lanes for g in range(half, left)])
        for copy in copies(stage, c):
            copy.start()
        for first in range(0, per_chunk, lanes_at_once):
            lanes = range(first, min(per_chunk, first + lanes_at_once))
            held = [(lane, g, value(lane, g)) for lane in lanes for g in range(half)]
            for lane, g, tile in held:
                kept[c * per_chunk + lane, g] = tile

    def step_body(step, _):
        @pl.when((step < chunks) & (step % begin_chunks == 0))
        def _():
            begin(step)

        for stage in range(stages, 0, -1):
            c = step - stage * lag

            @pl.when((c >= 0) & (c < chunks))
            def _(stage=stage, c=c):
                advance(stage, c)

        return 0

    lax.fori_loop(0, chunks + stages * lag, step_body, 0)
    for v in range(0, blocks, sublanes):
        out_ref[:, v : v + sublanes, :] = jnp.swapaxes(kept[v : v + sublanes, 0], 0, 1)


def per_device(intensity, counts, segment_ids, tile_ids, block_order, tiles):
    angles, rows, width = intensity.shape
    edge = tiles.shape[1]
    segments = width // edge
    groups = lax.axis_size("angle")
    cores = lax.axis_size("tile")
    stages = groups.bit_length() - 1
    capacity = 2 * rows // groups
    blocks = block_order.shape[0] // cores
    chunks = math.gcd(chunk_total, blocks)
    per_chunk = blocks // chunks
    forward, inverse, powers = filter_tables(rows, edge)

    smem = pl.BlockSpec(memory_space=pltpu.SMEM)
    vmem = pl.BlockSpec(memory_space=pltpu.VMEM)
    hbm = pl.BlockSpec(memory_space=pltpu.HBM)
    dma = pltpu.SemaphoreType.DMA
    f32, bf16 = jnp.float32, jnp.bfloat16
    together = math.gcd(angles, 2)
    plane = pltpu.VMEM((together, segments * (edge + pitch_extra), rows), f32)
    halves = [groups >> (stage + 1) for stage in range(stages)]
    data = [pltpu.VMEM((chunks, per_chunk, half, capacity, edge), jnp.int16) for half in halves]
    unit = [pltpu.VMEM((chunks, per_chunk * half, edge), f32) for half in halves]
    volume = pl.pallas_call(
        functools.partial(whole_kernel, stages, cores, chunks),
        out_shape=jax.ShapeDtypeStruct((capacity, blocks, edge), f32),
        in_specs=[smem] * 4 + [hbm] * 5,
        out_specs=vmem,
        scratch_shapes=[
            pltpu.VMEM(intensity.shape, f32),
            pltpu.VMEM(forward.shape, bf16),
            pltpu.VMEM(inverse.shape, bf16),
            pltpu.VMEM(powers.shape, f32),
            pltpu.VMEM(tiles.shape, bf16),
            plane, plane, plane,
            pltpu.VMEM((together, 2, segments, rows), f32),
            pltpu.VMEM((angles, segments, rows, edge), bf16),
            pltpu.VMEM((cores - 1, angles, segments, rows, edge), bf16),
            pltpu.SMEM((groups,), jnp.int32),
            pltpu.VMEM((math.gcd(chunks, 2) * per_chunk, rows + capacity, edge), f32),
            pltpu.VMEM((blocks, groups // 2, capacity, edge), f32),
            dma((angles,)),
            dma((4,)),
            dma((cores - 1, angles)),
            dma((cores - 1, angles)),
            dma((stages, chunks)),
            dma((stages, chunks)),
            dma((stages, chunks)),
            dma((stages, chunks)),
            *data, *data, *unit, *unit,
        ],
        compiler_params=pltpu.CompilerParams(
            vmem_limit_bytes=60 * 2**20, collective_id=0, has_side_effects=True
        ),
        name="tomography",
    )(
        counts, segment_ids, tile_ids, block_order, intensity,
        jnp.asarray(forward), jnp.asarray(inverse), jnp.asarray(powers), tiles,
    )
    return volume[None]


def solution(mesh):
    in_specs = (P(("groups", "angle", "tile"), None, None), P("groups"), P(), P(), P("groups"), P())
    out_specs = P(("groups", "angle"), None, "tile", None)
    return jax.shard_map(
        per_device, mesh=mesh, in_specs=in_specs, out_specs=out_specs, check_vma=False
    )
```

```python
import functools
import math

import jax
import jax.numpy as jnp
import numpy as np
from jax import lax
from jax.experimental import pallas as pl
from jax.experimental.pallas import tpu as pltpu
from jax.sharding import PartitionSpec as P

paganin_alpha = 2.0
chunk_total = 8
sublanes = 8
lag = 3
code_top = 32760.0
round_shift = 12582912.0
MESH = pl.DeviceIdType.MESH
pitch_extra = 9


def split_pair(array):
    high = array.astype(jnp.bfloat16)
    low = (array - high.astype(jnp.float32)).astype(jnp.bfloat16)
    return high, low


def filter_tables(row_total, edge):
    index = np.arange(row_total)
    phase = 2.0 * np.pi * (index[:, None] * index[None, :] % row_total) / row_total
    hartley = (np.cos(phase) + np.sin(phase)) / math.sqrt(row_total)
    a = 1.0 + paganin_alpha * (4.0 * np.sin(np.pi * index / row_total) ** 2 + 2.0)
    pole = (a - np.sqrt(a * a - 4.0 * paganin_alpha**2)) / (2.0 * paganin_alpha)
    gain = pole / (paganin_alpha * (1.0 - pole * pole))

    def halves(matrix):
        high = matrix.astype(np.float32).astype(jnp.bfloat16)
        return high, (matrix - high.astype(np.float64)).astype(np.float32).astype(jnp.bfloat16)

    high, low = halves(hartley * gain[None, :])
    forward = np.concatenate([np.concatenate([high, low], 1)] * 2, 0)
    high, low = halves(hartley)
    inverse = np.concatenate([np.concatenate([high, high], 1), np.concatenate([low, low], 1)], 0)
    reach = pole[None, :] ** np.arange(1, edge + 1)[:, None]
    powers = np.concatenate([reach, reach[::-1]], 0).astype(np.float32)
    return forward, inverse, powers


def filter_one(x_ref, forward_ref, inverse_ref, power_ref, out_ref, spectrum, ahead_ref, behind_ref, ends):
    segments, rows, edge = out_ref.shape
    pitch = edge + pitch_extra
    for s in range(segments):
        high, low = split_pair(x_ref[:, s * edge : (s + 1) * edge])
        both = jnp.concatenate([high, low], axis=0)
        product = lax.dot_general(
            both, forward_ref[...], (((0,), (0,)), ((), ())), preferred_element_type=jnp.float32
        )
        spectrum[s * pitch : s * pitch + edge, :] = product[:, :rows] + product[:, rows:]
    pole = jnp.broadcast_to(power_ref[0:1, :], (segments, rows))
    zero = jnp.zeros((segments, rows), jnp.float32)

    def column(t):
        return pl.ds(t, segments, stride=pitch)

    def sweep(t, state):
        ahead, behind = state
        ahead = ahead * pole + spectrum[column(t), :]
        ahead_ref[column(t), :] = ahead
        back = edge - 1 - t
        behind = behind * pole
        behind_ref[column(back), :] = behind
        return ahead, behind + spectrum[column(back), :]

    ahead, behind = lax.fori_loop(0, edge, sweep, (zero, zero), unroll=16)
    ends[0] = ahead
    ends[1] = behind
    for s in range(segments):
        span = slice(s * pitch, s * pitch + edge)
        before, after = (s - 1) % segments, (s + 1) % segments
        value = ahead_ref[span, :] + behind_ref[span, :]
        value = value + power_ref[:edge, :] * ends[0, before : before + 1, :]
        value = value + power_ref[edge:, :] * ends[1, after : after + 1, :]
        high, low = split_pair(value)
        both = jnp.concatenate([high, low], axis=1)
        product = lax.dot_general(
            inverse_ref[...], both, (((1,), (1,)), ((), ())), preferred_element_type=jnp.float32
        )
        out_ref[s] = (-jnp.log(product[:rows] + product[rows:])).astype(jnp.bfloat16)


def encode(value):
    top = jnp.maximum(jnp.max(jnp.abs(value), axis=0, keepdims=True), 1e-30)
    scaled = value * (code_top / top)
    code = (scaled + round_shift) - round_shift
    return code.astype(jnp.int32).astype(jnp.int16), top * (1.0 / code_top)


def decode(code, unit):
    return code.astype(jnp.int32).astype(jnp.float32) * unit


def whole_kernel(
    stages, cores, chunks, count_ref, seg_ref, tile_ref, order_ref, x_hbm, forward_hbm, inverse_hbm,
    power_hbm, tiles_hbm, out_ref, x_buf, forward_ref, inverse_ref, power_ref, tiles_ref, spectrum,
    ahead_ref, behind_ref, ends, own, other, start_ref, rows_ref, kept, x_sem, load_sem, swap_send,
    swap_recv, data_send, data_recv, unit_send, unit_recv, *buffers
):
    send, came, send_unit, came_unit = (buffers[i * stages : (i + 1) * stages] for i in range(4))
    groups = 2**stages
    angles, _, rows, edge = own.shape
    capacity, blocks, _ = out_ref.shape
    per_chunk = blocks // chunks
    place, core = lax.axis_index("angle"), lax.axis_index("tile")

    loads = [
        pltpu.make_async_copy(source, target, load_sem.at[i])
        for i, (source, target) in enumerate(
            (
                (forward_hbm, forward_ref),
                (power_hbm, power_ref),
                (inverse_hbm, inverse_ref),
                (tiles_hbm, tiles_ref),
            )
        )
    ]

    def projection(a):
        return pltpu.make_async_copy(x_hbm.at[a], x_buf.at[a], x_sem.at[a])

    projection(0).start()
    for load in loads[:3]:
        load.start()
    for a in range(1, angles):
        projection(a).start()
    loads[3].start()

    def across(bit):
        return place + (1 - 2 * ((place // (1 << bit)) % 2)) * (1 << bit)

    partners = [across(bit) for bit in range(stages)]
    neighbours = [lax.rem(core + step, cores) for step in range(1, cores)]
    barrier = pltpu.get_barrier_semaphore()
    for partner in partners:
        pl.semaphore_signal(barrier, inc=1, device_id={"angle": partner}, device_id_type=MESH)
    for neighbour in neighbours:
        pl.semaphore_signal(barrier, inc=1, device_id={"tile": neighbour}, device_id_type=MESH)

    running = jnp.int32(0)
    for g in range(groups):
        start_ref[g] = running
        running = running + count_ref[g]
    for lane in range(per_chunk):
        rows_ref[lane, rows:, :] = jnp.zeros((capacity, edge), jnp.float32)
    for load in loads[:3]:
        load.wait()

    def swap(index, a):
        return pltpu.make_async_remote_copy(
            src_ref=own.at[a],
            dst_ref=other.at[index, a],
            send_sem=swap_send.at[index, a],
            recv_sem=swap_recv.at[index, a],
            device_id={"tile": neighbours[index]},
            device_id_type=MESH,
        )

    def filter_angle(a, _):
        projection(a).wait()
        filter_one(
            x_buf.at[a], forward_ref, inverse_ref, power_ref, own.at[a],
            spectrum, ahead_ref, behind_ref, ends,
        )

        @pl.when(a == 0)
        def _():
            pl.semaphore_wait(barrier, stages + cores - 1)

        for index in range(cores - 1):
            swap(index, a).start()
        return 0

    lax.fori_loop(0, angles, filter_angle, 0)
    loads[3].wait()
    for index in range(cores - 1):
        for a in range(angles):
            swap(index, a).wait()

    slot = lax.broadcasted_iota(jnp.int32, (capacity, edge), 0)
    thick_rows = [(lambda a, s: own[a, s], (place * cores + core) * angles)]
    for index in range(cores - 1):
        source = lax.rem(core + cores - 1 - index, cores)
        thick_rows.append(
            (lambda a, s, index=index: other[index, a, s], (place * cores + source) * angles)
        )

    def project(v):
        block = order_ref[core * blocks + v]
        pieces, maps = [], []
        for thick, first_row in thick_rows:
            for a in range(angles):
                pieces.append(thick(a, seg_ref[first_row + a, block]))
                maps.append(tiles_ref[tile_ref[first_row + a, block]])
        return jnp.dot(
            jnp.concatenate(pieces, axis=1),
            jnp.concatenate(maps, axis=0),
            preferred_element_type=jnp.float32,
        )

    def variant_of(c):
        return 1 - ((c + 2) % 4) // 3 if stages > 1 else 0

    def owner(variant, position):
        group = place
        for i in range(stages):
            if (position >> (stages - 1 - i)) & 1:
                move = partners[i] - place
                if stages > 1 and i < 2:
                    move = move * (1 - variant) + (partners[1 - i] - place) * variant
                group = group + move
        return group

    def copies(stage, c):
        partner = partners[stage]
        if stages > 1 and stage < 2:
            variant = variant_of(c)
            partner = partners[stage] * (1 - variant) + partners[1 - stage] * variant
        made = []
        for source, target, sent, got in (
            (send[stage], came[stage], data_send, data_recv),
            (send_unit[stage], came_unit[stage], unit_send, unit_recv),
        ):
            made.append(
                pltpu.make_async_remote_copy(
                    src_ref=source.at[c],
                    dst_ref=target.at[c],
                    send_sem=sent.at[stage, c],
                    recv_sem=got.at[stage, c],
                    device_id={"angle": partner},
                    device_id_type=MESH,
                )
            )
        return made

    def ship(stage, c, tiles_out):
        half = groups >> (stage + 1)
        coded = [(lane, g, *encode(value)) for lane, g, value in tiles_out]
        for lane, g, code, unit in coded:
            row = lane * half + g - half
            send[stage][c, lane, g - half] = code
            send_unit[stage][c, row : row + 1, :] = unit

    def begin(c):
        variant = variant_of(c)
        for lane in range(per_chunk):
            rows_ref[lane, :rows, :] = project(c * per_chunk + lane)
        spans = [owner(variant, g) for g in range(groups)]
        spans = [(start_ref[group], slot < count_ref[group]) for group in spans]

        def picked(lane, g):
            start, inside = spans[g]
            return jnp.where(inside, rows_ref[lane, pl.ds(start, capacity), :], 0.0)

        for lane in range(per_chunk):
            ship(0, c, [(lane, g, picked(lane, g)) for g in range(groups // 2, groups)])
        for copy in copies(0, c):
            copy.start()
        for lane in range(per_chunk):
            held = [picked(lane, g) for g in range(groups // 2)]
            for g, value in enumerate(held):
                kept[c * per_chunk + lane, g] = value

    def advance(stage, c):
        for copy in copies(stage - 1, c):
            copy.wait()
        left = groups >> stage

        def value(lane, g):
            unit = came_unit[stage - 1][c, lane * left + g : lane * left + g + 1, :]
            return kept[c * per_chunk + lane, g] + decode(came[stage - 1][c, lane, g], unit)

        if stage == stages:
            for lane, last in enumerate([value(lane, 0) for lane in range(per_chunk)]):
                kept[c * per_chunk + lane, 0] = last
            return
        half = left // 2
        lanes_at_once = max(1, 4 // half)
        for first in range(0, per_chunk, lanes_at_once):
            lanes = range(first, min(per_chunk, first + lanes_at_once))
            ship(stage, c, [(lane, g, value(lane, g)) for lane in lanes for g in range(half, left)])
        for copy in copies(stage, c):
            copy.start()
        for first in range(0, per_chunk, lanes_at_once):
            lanes = range(first, min(per_chunk, first + lanes_at_once))
            held = [(lane, g, value(lane, g)) for lane in lanes for g in range(half)]
            for lane, g, tile in held:
                kept[c * per_chunk + lane, g] = tile

    def step_body(step, _):
        @pl.when(step < chunks)
        def _():
            begin(step)

        for stage in range(stages, 0, -1):
            c = step - stage * lag

            @pl.when((c >= 0) & (c < chunks))
            def _(stage=stage, c=c):
                advance(stage, c)

        return 0

    lax.fori_loop(0, chunks + stages * lag, step_body, 0)
    for v in range(0, blocks, sublanes):
        out_ref[:, v : v + sublanes, :] = jnp.swapaxes(kept[v : v + sublanes, 0], 0, 1)


def per_device(intensity, counts, segment_ids, tile_ids, block_order, tiles):
    angles, rows, width = intensity.shape
    edge = tiles.shape[1]
    segments = width // edge
    groups = lax.axis_size("angle")
    cores = lax.axis_size("tile")
    stages = groups.bit_length() - 1
    capacity = 2 * rows // groups
    blocks = block_order.shape[0] // cores
    chunks = math.gcd(chunk_total, blocks)
    per_chunk = blocks // chunks
    forward, inverse, powers = filter_tables(rows, edge)

    smem = pl.BlockSpec(memory_space=pltpu.SMEM)
    vmem = pl.BlockSpec(memory_space=pltpu.VMEM)
    hbm = pl.BlockSpec(memory_space=pl.ANY)
    dma = pltpu.SemaphoreType.DMA
    f32, bf16 = jnp.float32, jnp.bfloat16
    plane = pltpu.VMEM((segments * (edge + pitch_extra), rows), f32)
    halves = [groups >> (stage + 1) for stage in range(stages)]
    data = [pltpu.VMEM((chunks, per_chunk, half, capacity, edge), jnp.int16) for half in halves]
    unit = [pltpu.VMEM((chunks, per_chunk * half, edge), f32) for half in halves]
    volume = pl.pallas_call(
        functools.partial(whole_kernel, stages, cores, chunks),
        out_shape=jax.ShapeDtypeStruct((capacity, blocks, edge), f32),
        in_specs=[smem] * 4 + [hbm] * 5,
        out_specs=vmem,
        scratch_shapes=[
            pltpu.VMEM(intensity.shape, f32),
            pltpu.VMEM(forward.shape, bf16),
            pltpu.VMEM(inverse.shape, bf16),
            pltpu.VMEM(powers.shape, f32),
            pltpu.VMEM(tiles.shape, bf16),
            plane, plane, plane,
            pltpu.VMEM((2, segments, rows), f32),
            pltpu.VMEM((angles, segments, rows, edge), bf16),
            pltpu.VMEM((cores - 1, angles, segments, rows, edge), bf16),
            pltpu.SMEM((groups,), jnp.int32),
            pltpu.VMEM((per_chunk, rows + capacity, edge), f32),
            pltpu.VMEM((blocks, groups // 2, capacity, edge), f32),
            dma((angles,)),
            dma((4,)),
            dma((cores - 1, angles)),
            dma((cores - 1, angles)),
            dma((stages, chunks)),
            dma((stages, chunks)),
            dma((stages, chunks)),
            dma((stages, chunks)),
            *data, *data, *unit, *unit,
        ],
        compiler_params=pltpu.CompilerParams(
            vmem_limit_bytes=51 * 2**20, collective_id=0, has_side_effects=True
        ),
        name="tomography",
    )(
        counts, segment_ids, tile_ids, block_order, intensity,
        jnp.asarray(forward), jnp.asarray(inverse), jnp.asarray(powers), tiles,
    )
    return volume[None]


def solution(mesh):
    in_specs = (P(("groups", "angle", "tile"), None, None), P("groups"), P(), P(), P("groups"), P())
    out_specs = P(("groups", "angle"), None, "tile", None)
    return jax.shard_map(
        per_device, mesh=mesh, in_specs=in_specs, out_specs=out_specs, check_vma=False
    )
```

```python
import functools
import math

import jax
import jax.numpy as jnp
import numpy as np
from jax import lax
from jax.experimental import pallas as pl
from jax.experimental.pallas import tpu as pltpu
from jax.sharding import PartitionSpec as P

paganin_alpha = 2.0
chunk_total = 8
sublanes = 8
lag = 3
code_top = 32760.0
round_shift = 12582912.0
MESH = pl.DeviceIdType.MESH
pitch_extra = 9


def split_pair(array):
    high = array.astype(jnp.bfloat16)
    low = (array - high.astype(jnp.float32)).astype(jnp.bfloat16)
    return high, low


def filter_tables(row_total, edge):
    index = np.arange(row_total)
    phase = 2.0 * np.pi * (index[:, None] * index[None, :] % row_total) / row_total
    hartley = (np.cos(phase) + np.sin(phase)) / math.sqrt(row_total)
    a = 1.0 + paganin_alpha * (4.0 * np.sin(np.pi * index / row_total) ** 2 + 2.0)
    pole = (a - np.sqrt(a * a - 4.0 * paganin_alpha**2)) / (2.0 * paganin_alpha)
    gain = pole / (paganin_alpha * (1.0 - pole * pole))

    def halves(matrix):
        high = matrix.astype(np.float32).astype(jnp.bfloat16)
        return high, (matrix - high.astype(np.float64)).astype(np.float32).astype(jnp.bfloat16)

    high, low = halves(hartley * gain[None, :])
    forward = np.concatenate([np.concatenate([high, low], 1)] * 2, 0)
    high, low = halves(hartley)
    inverse = np.concatenate([np.concatenate([high, high], 1), np.concatenate([low, low], 1)], 0)
    reach = pole[None, :] ** np.arange(1, edge + 1)[:, None]
    powers = np.concatenate([reach, reach[::-1]], 0).astype(np.float32)
    return forward, inverse, powers


def filter_one(x_ref, forward_ref, inverse_ref, power_ref, out_ref, spectrum, ahead_ref, behind_ref, ends):
    segments, rows, edge = out_ref.shape
    pitch = edge + pitch_extra
    for s in range(segments):
        high, low = split_pair(x_ref[:, s * edge : (s + 1) * edge])
        both = jnp.concatenate([high, low], axis=0)
        product = lax.dot_general(
            both, forward_ref[...], (((0,), (0,)), ((), ())), preferred_element_type=jnp.float32
        )
        spectrum[s * pitch : s * pitch + edge, :] = product[:, :rows] + product[:, rows:]
    pole = jnp.broadcast_to(power_ref[0:1, :], (segments, rows))
    zero = jnp.zeros((segments, rows), jnp.float32)

    def column(t):
        return pl.ds(t, segments, stride=pitch)

    def sweep(t, state):
        ahead, behind = state
        ahead = ahead * pole + spectrum[column(t), :]
        ahead_ref[column(t), :] = ahead
        back = edge - 1 - t
        behind = behind * pole
        behind_ref[column(back), :] = behind
        return ahead, behind + spectrum[column(back), :]

    ahead, behind = lax.fori_loop(0, edge, sweep, (zero, zero), unroll=16)
    ends[0] = ahead
    ends[1] = behind
    for s in range(segments):
        span = slice(s * pitch, s * pitch + edge)
        before, after = (s - 1) % segments, (s + 1) % segments
        value = ahead_ref[span, :] + behind_ref[span, :]
        value = value + power_ref[:edge, :] * ends[0, before : before + 1, :]
        value = value + power_ref[edge:, :] * ends[1, after : after + 1, :]
        high, low = split_pair(value)
        both = jnp.concatenate([high, low], axis=1)
        product = lax.dot_general(
            inverse_ref[...], both, (((1,), (1,)), ((), ())), preferred_element_type=jnp.float32
        )
        out_ref[s] = (-jnp.log(product[:rows] + product[rows:])).astype(jnp.bfloat16)


def encode(value):
    top = jnp.maximum(jnp.max(jnp.abs(value), axis=0, keepdims=True), 1e-30)
    scaled = value * (code_top / top)
    code = (scaled + round_shift) - round_shift
    return code.astype(jnp.int32).astype(jnp.int16), top * (1.0 / code_top)


def decode(code, unit):
    return code.astype(jnp.int32).astype(jnp.float32) * unit


def whole_kernel(
    stages, cores, chunks, count_ref, seg_ref, tile_ref, order_ref, x_hbm, forward_hbm, inverse_hbm,
    power_hbm, tiles_hbm, out_ref, x_buf, forward_ref, inverse_ref, power_ref, tiles_ref, spectrum,
    ahead_ref, behind_ref, ends, own, other, start_ref, rows_ref, kept, x_sem, load_sem, swap_send,
    swap_recv, data_send, data_recv, unit_send, unit_recv, *buffers
):
    send, came, send_unit, came_unit = (buffers[i * stages : (i + 1) * stages] for i in range(4))
    groups = 2**stages
    angles, _, rows, edge = own.shape
    capacity, blocks, _ = out_ref.shape
    per_chunk = blocks // chunks
    place, core = lax.axis_index("angle"), lax.axis_index("tile")

    loads = [
        pltpu.make_async_copy(source, target, load_sem.at[i])
        for i, (source, target) in enumerate(
            (
                (forward_hbm, forward_ref),
                (power_hbm, power_ref),
                (inverse_hbm, inverse_ref),
                (tiles_hbm, tiles_ref),
            )
        )
    ]

    def projection(a):
        return pltpu.make_async_copy(x_hbm.at[a], x_buf.at[a], x_sem.at[a])

    projection(0).start()
    for load in loads[:3]:
        load.start()
    for a in range(1, angles):
        projection(a).start()
    loads[3].start()

    def across(bit):
        return place + (1 - 2 * ((place // (1 << bit)) % 2)) * (1 << bit)

    partners = [across(bit) for bit in range(stages)]
    neighbours = [lax.rem(core + step, cores) for step in range(1, cores)]
    barrier = pltpu.get_barrier_semaphore()
    for partner in partners:
        pl.semaphore_signal(barrier, inc=1, device_id={"angle": partner}, device_id_type=MESH)
    for neighbour in neighbours:
        pl.semaphore_signal(barrier, inc=1, device_id={"tile": neighbour}, device_id_type=MESH)

    running = jnp.int32(0)
    for g in range(groups):
        start_ref[g] = running
        running = running + count_ref[g]
    for lane in range(per_chunk):
        rows_ref[lane, rows:, :] = jnp.zeros((capacity, edge), jnp.float32)
    for load in loads[:3]:
        load.wait()

    def swap(index, a):
        return pltpu.make_async_remote_copy(
            src_ref=own.at[a],
            dst_ref=other.at[index, a],
            send_sem=swap_send.at[index, a],
            recv_sem=swap_recv.at[index, a],
            device_id={"tile": neighbours[index]},
            device_id_type=MESH,
        )

    def filter_angle(a, _):
        projection(a).wait()
        filter_one(
            x_buf.at[a], forward_ref, inverse_ref, power_ref, own.at[a],
            spectrum, ahead_ref, behind_ref, ends,
        )

        @pl.when(a == 0)
        def _():
            pl.semaphore_wait(barrier, stages + cores - 1)

        for index in range(cores - 1):
            swap(index, a).start()
        return 0

    lax.fori_loop(0, angles, filter_angle, 0)
    loads[3].wait()
    for index in range(cores - 1):
        for a in range(angles):
            swap(index, a).wait()

    slot = lax.broadcasted_iota(jnp.int32, (capacity, edge), 0)
    thick_rows = [(lambda a, s: own[a, s], (place * cores + core) * angles)]
    for index in range(cores - 1):
        source = lax.rem(core + cores - 1 - index, cores)
        thick_rows.append(
            (lambda a, s, index=index: other[index, a, s], (place * cores + source) * angles)
        )

    def project(v):
        block = order_ref[core * blocks + v]
        pieces, maps = [], []
        for thick, first_row in thick_rows:
            for a in range(angles):
                pieces.append(thick(a, seg_ref[first_row + a, block]))
                maps.append(tiles_ref[tile_ref[first_row + a, block]])
        return jnp.dot(
            jnp.concatenate(pieces, axis=1),
            jnp.concatenate(maps, axis=0),
            preferred_element_type=jnp.float32,
        )

    def variant_of(c):
        return ((c + 2) % 4) // 3 if stages > 1 else 0

    def owner(variant, position):
        group = place
        for i in range(stages):
            if (position >> (stages - 1 - i)) & 1:
                move = partners[i] - place
                if stages > 1 and i < 2:
                    move = move * (1 - variant) + (partners[1 - i] - place) * variant
                group = group + move
        return group

    def copies(stage, c):
        partner = partners[stage]
        if stages > 1 and stage < 2:
            variant = variant_of(c)
            partner = partners[stage] * (1 - variant) + partners[1 - stage] * variant
        made = []
        for source, target, sent, got in (
            (send[stage], came[stage], data_send, data_recv),
            (send_unit[stage], came_unit[stage], unit_send, unit_recv),
        ):
            made.append(
                pltpu.make_async_remote_copy(
                    src_ref=source.at[c],
                    dst_ref=target.at[c],
                    send_sem=sent.at[stage, c],
                    recv_sem=got.at[stage, c],
                    device_id={"angle": partner},
                    device_id_type=MESH,
                )
            )
        return made

    def ship(stage, c, tiles_out):
        half = groups >> (stage + 1)
        coded = [(lane, g, *encode(value)) for lane, g, value in tiles_out]
        for lane, g, code, unit in coded:
            row = lane * half + g - half
            send[stage][c, lane, g - half] = code
            send_unit[stage][c, row : row + 1, :] = unit

    def begin(c):
        variant = variant_of(c)
        for lane in range(per_chunk):
            rows_ref[lane, :rows, :] = project(c * per_chunk + lane)
        spans = [owner(variant, g) for g in range(groups)]
        spans = [(start_ref[group], slot < count_ref[group]) for group in spans]

        def picked(lane, g):
            start, inside = spans[g]
            return jnp.where(inside, rows_ref[lane, pl.ds(start, capacity), :], 0.0)

        for lane in range(per_chunk):
            ship(0, c, [(lane, g, picked(lane, g)) for g in range(groups // 2, groups)])
        for copy in copies(0, c):
            copy.start()
        for lane in range(per_chunk):
            held = [picked(lane, g) for g in range(groups // 2)]
            for g, value in enumerate(held):
                kept[c * per_chunk + lane, g] = value

    def advance(stage, c):
        for copy in copies(stage - 1, c):
            copy.wait()
        left = groups >> stage

        def value(lane, g):
            unit = came_unit[stage - 1][c, lane * left + g : lane * left + g + 1, :]
            return kept[c * per_chunk + lane, g] + decode(came[stage - 1][c, lane, g], unit)

        if stage == stages:
            for lane, last in enumerate([value(lane, 0) for lane in range(per_chunk)]):
                kept[c * per_chunk + lane, 0] = last
            return
        half = left // 2
        lanes_at_once = max(1, 4 // half)
        for first in range(0, per_chunk, lanes_at_once):
            lanes = range(first, min(per_chunk, first + lanes_at_once))
            ship(stage, c, [(lane, g, value(lane, g)) for lane in lanes for g in range(half, left)])
        for copy in copies(stage, c):
            copy.start()
        for first in range(0, per_chunk, lanes_at_once):
            lanes = range(first, min(per_chunk, first + lanes_at_once))
            held = [(lane, g, value(lane, g)) for lane in lanes for g in range(half)]
            for lane, g, tile in held:
                kept[c * per_chunk + lane, g] = tile

    def step_body(step, _):
        @pl.when(step < chunks)
        def _():
            begin(step)

        for stage in range(stages, 0, -1):
            c = step - stage * lag

            @pl.when((c >= 0) & (c < chunks))
            def _(stage=stage, c=c):
                advance(stage, c)

        return 0

    lax.fori_loop(0, chunks + stages * lag, step_body, 0)
    for v in range(0, blocks, sublanes):
        out_ref[:, v : v + sublanes, :] = jnp.swapaxes(kept[v : v + sublanes, 0], 0, 1)


def per_device(intensity, counts, segment_ids, tile_ids, block_order, tiles):
    angles, rows, width = intensity.shape
    edge = tiles.shape[1]
    segments = width // edge
    groups = lax.axis_size("angle")
    cores = lax.axis_size("tile")
    stages = groups.bit_length() - 1
    capacity = 2 * rows // groups
    blocks = block_order.shape[0] // cores
    chunks = math.gcd(chunk_total, blocks)
    per_chunk = blocks // chunks
    forward, inverse, powers = filter_tables(rows, edge)

    smem = pl.BlockSpec(memory_space=pltpu.SMEM)
    vmem = pl.BlockSpec(memory_space=pltpu.VMEM)
    hbm = pl.BlockSpec(memory_space=pl.ANY)
    dma = pltpu.SemaphoreType.DMA
    f32, bf16 = jnp.float32, jnp.bfloat16
    plane = pltpu.VMEM((segments * (edge + pitch_extra), rows), f32)
    halves = [groups >> (stage + 1) for stage in range(stages)]
    data = [pltpu.VMEM((chunks, per_chunk, half, capacity, edge), jnp.int16) for half in halves]
    unit = [pltpu.VMEM((chunks, per_chunk * half, edge), f32) for half in halves]
    volume = pl.pallas_call(
        functools.partial(whole_kernel, stages, cores, chunks),
        out_shape=jax.ShapeDtypeStruct((capacity, blocks, edge), f32),
        in_specs=[smem] * 4 + [hbm] * 5,
        out_specs=vmem,
        scratch_shapes=[
            pltpu.VMEM(intensity.shape, f32),
            pltpu.VMEM(forward.shape, bf16),
            pltpu.VMEM(inverse.shape, bf16),
            pltpu.VMEM(powers.shape, f32),
            pltpu.VMEM(tiles.shape, bf16),
            plane, plane, plane,
            pltpu.VMEM((2, segments, rows), f32),
            pltpu.VMEM((angles, segments, rows, edge), bf16),
            pltpu.VMEM((cores - 1, angles, segments, rows, edge), bf16),
            pltpu.SMEM((groups,), jnp.int32),
            pltpu.VMEM((per_chunk, rows + capacity, edge), f32),
            pltpu.VMEM((blocks, groups // 2, capacity, edge), f32),
            dma((angles,)),
            dma((4,)),
            dma((cores - 1, angles)),
            dma((cores - 1, angles)),
            dma((stages, chunks)),
            dma((stages, chunks)),
            dma((stages, chunks)),
            dma((stages, chunks)),
            *data, *data, *unit, *unit,
        ],
        compiler_params=pltpu.CompilerParams(
            vmem_limit_bytes=60 * 2**20, collective_id=0, has_side_effects=True
        ),
        name="tomography",
    )(
        counts, segment_ids, tile_ids, block_order, intensity,
        jnp.asarray(forward), jnp.asarray(inverse), jnp.asarray(powers), tiles,
    )
    return volume[None]


def solution(mesh):
    in_specs = (P(("groups", "angle", "tile"), None, None), P("groups"), P(), P(), P("groups"), P())
    out_specs = P(("groups", "angle"), None, "tile", None)
    return jax.shard_map(
        per_device, mesh=mesh, in_specs=in_specs, out_specs=out_specs, check_vma=False
    )
```
